32 devices in a mesh: groups: 2 (over y), ctx: 2 (over x), exp: 4 (over z), tp: 2 (over core).
Axes of the slice: x: 2, y: 2, z: 4, core: 2. Of those that a mesh axis runs over, the one named last changes fastest.
Arguments:
- queries: bfloat16 [512, 8192], P(('groups', 'ctx'), ('exp', 'tp')), parts along dimension 0, may hold values from -6 to 6
- keys: bfloat16 [512, 8192], P(('groups', 'ctx'), ('exp', 'tp')), parts along dimension 0, may hold values from -6 to 6
- values: bfloat16 [512, 8192], P(('groups', 'ctx'), ('exp', 'tp')), parts along dimension 0, may hold values from -6 to 6
- log_decay: float32 [512, 64], P(('groups', 'ctx'), ('exp', 'tp')), parts along dimension 0, may hold values from -1 to 0
- moe_input: bfloat16 [64, 6144], P(('groups', 'ctx', 'exp'), 'tp'), parts along dimension 0, may hold values from -6 to 6
- route_ids: int32 [64, 2], P(('groups', 'ctx', 'exp')), parts along dimension 0, may hold values from 0 to 3, all different within a row; in each aligned block of 4 rows (0 to 3, 4 to 7, ...) at most 3 rows name the same one
- route_weight: float32 [64, 2], P(('groups', 'ctx', 'exp')), parts along dimension 0, may hold values from 0.2 to 1
- gate_up: bfloat16 [4, 6144, 2, 4608], P('exp', 'tp', None, 'ctx'), may hold values from -0.078125 to 0.078125
- down: bfloat16 [4, 4608, 6144], P('exp', None, ('tp', 'ctx')), may hold values from -0.09375 to 0.09375
Outputs:
- attended: bfloat16 [512, 8192], P(('groups', 'ctx'), ('exp', 'tp')), parts along dimension 0
- moe_out: bfloat16 [64, 6144], P(('groups', 'ctx', 'exp'), 'tp'), parts along dimension 0
The draws below stay inside these ranges and needn't reach their ends.
There are 2 independent parts, one for each index of `groups`. The reference program is written for one: setup_inputs(seed, part) draws one part's arguments, and reference() takes and returns one part's arrays. A program takes and returns all parts, laid end to end along the dimension named above; an argument that names none is the same for every part. Nothing has to cross between parts.
Inputs may be any that keep to these rules, and one draw needn't show every extreme that they name: `route_ids`: each row names two different experts. In each aligned block of 4 rows (the rows of one device) no expert is named more than 3 times, and some block names one expert exactly 3 times.
All inputs are finite; a program needn't handle non-finite values.
Results may differ from the reference program's by a relative error of at most 0.023.
Values may be sent and summed in bfloat16 or wider, within the bound.
No kernel may reach another device: no remote copies, remote signals or barrier semaphores. Data moves between devices by JAX's collectives and lax.ppermute only.
A program may use at most 128 MiB of HBM per device.

```python
import math
import jax
import jax.numpy as jnp
import numpy as np
from jax import lax

HEADS = 64
DH = 128
D = 6144
FF = 4608
TOK_DEV = 128
MOE_DEV = 4
SEQUENCE_LENGTH = 256
EXPERTS = 4
MTOK = 32
CAP = 3
N_CTX = 2
N_EXP = 4


def draw_log_decay(key, part):
    key = jax.random.fold_in(key, 7)
    k_rate, k_jit, source_index, k_amt = jax.random.split(key, 4)
    slow = 0.3 / SEQUENCE_LENGTH
    spread = jax.random.uniform(k_rate, (HEADS,), jnp.float32)
    fading_speed = jnp.exp(jnp.log(slow) + spread * (jnp.log(0.04) - jnp.log(slow)))
    noise_offset = jnp.exp(jax.random.uniform(k_jit, (SEQUENCE_LENGTH, HEADS), jnp.float32, -0.7, 0.7))
    abrupt_spike = jax.random.uniform(source_index, (SEQUENCE_LENGTH, 1), jnp.float32) < 3.0 / SEQUENCE_LENGTH
    fading_factor = jnp.log(jax.random.uniform(k_amt, (SEQUENCE_LENGTH, HEADS), jnp.float32, 0.5, 0.8))
    return -fading_speed[None, :] * noise_offset + jnp.where(abrupt_spike, fading_factor, 0.0)


def shard_levels(own_key, dims, pieces, low, high):
    level, own = 1.0, jax.random.fold_in(own_key, 6)
    for dim, blocks in pieces:
        steps = jnp.exp(jax.random.uniform(jax.random.fold_in(own, dim), (blocks,), jnp.float32, low / len(pieces), high / len(pieces)))
        level = level * jnp.repeat(steps, dims[dim] // blocks).reshape([-1 if axis == dim else 1 for axis in range(len(dims))])
    return level


def routed_block(key, own, number, rows, count, top, most, lean):
    order = jax.random.permutation(key, count)
    heavy_load, common = portions_of(count, rows * top, most, lean, True), portions_of(count, rows * top, most, lean, False)
    places = jnp.arange(count)

    def named(lengths, offset_by):
        used = int((lengths > 0).sum())
        fixed = max(1, used // 4)
        passed = fixed + (places - fixed + offset_by * (used - fixed)) % max(1, count - fixed)
        return jnp.zeros((count,), jnp.int32).at[order[jnp.where(places < fixed, places, passed)]].set(jnp.asarray(lengths, jnp.int32))

    lengths = jnp.where(number % 4 == 0, named(heavy_load, number // 4), named(common, number - number // 4 - 1))
    mixed = jax.random.permutation(jax.random.fold_in(own, 3), count)
    donor, taker = mixed[0:count // 2 * 2:2], mixed[1:count // 2 * 2:2]
    room = jnp.minimum(lengths[donor] - 1, most - lengths[taker]) // 2
    room = jnp.where((donor == order[0]) | (taker == order[0]) | (lengths[taker] == 0), 0, jnp.maximum(room, 0))
    passed = jax.random.randint(jax.random.fold_in(own, 4), (count // 2,), 0, 1 << 20) % (room + 1)
    lengths = lengths.at[donor].add(-passed).at[taker].add(passed)
    items = jnp.searchsorted(jnp.cumsum(lengths), jnp.arange(rows * top), side="right").astype(jnp.int32)
    table = items.reshape(top, rows).T
    table = table[jax.random.permutation(jax.random.fold_in(own, 1), rows)]
    offset_by = jax.random.randint(jax.random.fold_in(own, 2), (rows, 1), 0, top)
    return jnp.take_along_axis(table, (jnp.arange(top)[None, :] + offset_by) % top, axis=1)


def portions_of(amount, total, reach, skew, full):
    weights = [(1 << 20) // math.isqrt(rank ** skew) + 1 for rank in range(1, amount + 1)]
    largest = reach if full else min(reach, max(-(-total // amount), total * weights[0] // sum(weights)))
    least = 1 if total - largest >= amount - 1 else 0
    holding, surplus = [largest] + [least] * (amount - 1), total - largest - least * (amount - 1)
    while surplus > 0:
        free = [i for i in range(1, amount) if holding[i] < largest] or [i for i in range(1, amount) if holding[i] < reach]
        whole, left = sum([weights[i] for i in free]), surplus
        for i in free:
            extra = min(reach - holding[i], max(1, left * weights[i] // whole), surplus)
            holding[i] = holding[i] + extra
            surplus = surplus - extra
    return np.array(holding)


def gaussian(stream_key, dims, width, most, cuts=(), held_as=jnp.bfloat16):
    factor_of = shard_levels(stream_key, dims, cuts, -0.22, 0.18) if cuts else 1.0
    entries = jax.random.normal(stream_key, dims, jnp.float32) * width * factor_of
    return jnp.minimum(jnp.maximum(entries, -most), most).astype(held_as)


def setup_inputs(seed: int = 0, part: int = 0) -> dict:
    splits = jax.random.split(jax.random.key(seed), 10)
    part_keys = jax.random.split(jax.random.fold_in(splits[9], part), 10)
    queries = gaussian(part_keys[0], (SEQUENCE_LENGTH, HEADS * DH), 1.0, 6.0, ((0, 2), (1, 8)))
    keys = gaussian(part_keys[1], (SEQUENCE_LENGTH, HEADS * DH), 1.0, 6.0, ((0, 2), (1, 8)))
    values = gaussian(part_keys[2], (SEQUENCE_LENGTH, HEADS * DH), 1.0, 6.0, ((0, 2), (1, 8)))
    log_decay = draw_log_decay(jax.random.fold_in(jax.random.fold_in(splits[9], part), 71), part)
    moe_input = gaussian(part_keys[4], (MTOK, D), 1.0, 6.0, ((0, 8), (1, 2)))
    route_ids_keys = jax.random.split(jax.random.fold_in(part_keys[5], 1), MTOK // MOE_DEV)
    route_ids_turns = jax.random.permutation(jax.random.fold_in(part_keys[5], 3), MTOK // MOE_DEV)
    route_ids = jax.vmap(lambda own, number: routed_block(jax.random.fold_in(part_keys[5], 2), own, number, MOE_DEV, EXPERTS, 2, CAP, 2))(route_ids_keys, route_ids_turns).reshape((MTOK, 2))
    route_weight = jnp.clip(0.2 + 0.8 * jax.random.uniform(part_keys[6], (MTOK, 2), jnp.float32) ** shard_levels(part_keys[6], (MTOK, 2), ((0, 8),), -0.2, 0.2), 0.2, 1.0)
    gate_up = gaussian(splits[7], (EXPERTS, D, 2, FF), D ** -0.5, 0.078125, ((0, 4), (1, 2), (3, 2)))
    down = gaussian(splits[8], (EXPERTS, FF, D), FF ** -0.5, 0.09375, ((0, 4), (2, 4)))
    return dict(queries=queries, keys=keys, values=values, log_decay=log_decay, moe_input=moe_input, route_ids=route_ids, route_weight=route_weight, gate_up=gate_up, down=down)


def attend_block(state, qb, kb, vb, lb):
    rows = qb.shape[0]
    cum = jnp.cumsum(lb, axis=0)
    diff = jnp.transpose(cum)[:, :, None] - jnp.transpose(cum)[:, None, :]
    causal = jnp.arange(rows)[:, None] >= jnp.arange(rows)[None, :]
    decay = jnp.where(causal[None, :, :], jnp.exp(jnp.minimum(diff, 0.0)), 0.0)
    scores = jnp.einsum('thd,shd->hts', qb.astype(jnp.float32), kb.astype(jnp.float32))
    weights = (scores * decay).astype(jnp.bfloat16)
    intra = jnp.einsum('hts,shd->thd', weights.astype(jnp.float32), vb.astype(jnp.float32))
    last = cum[-1]
    kscaled = kb.astype(jnp.float32) * jnp.exp(last[None, :] - cum)[:, :, None]
    local = jnp.einsum('shd,she->hde', kscaled, vb.astype(jnp.float32), precision=lax.Precision.HIGHEST)
    qscaled = qb.astype(jnp.float32) * jnp.exp(cum)[:, :, None]
    inter = jnp.einsum('thd,hde->the', qscaled, state, precision=lax.Precision.HIGHEST)
    mixed = intra + inter
    normed = mixed * lax.rsqrt(lax.optimization_barrier(jnp.mean(mixed * mixed, axis=-1, keepdims=True)) + 1e-06)
    new_state = jnp.exp(last)[:, None, None] * state + local
    return (new_state, normed.astype(jnp.bfloat16))

def reference(queries, keys, values, log_decay, moe_input, route_ids, route_weight, gate_up, down):
    shape = (N_CTX, TOK_DEV, HEADS, DH)
    qs = queries.reshape(shape)
    ks = keys.reshape(shape)
    vs = values.reshape(shape)
    ls = log_decay.reshape(N_CTX, TOK_DEV, HEADS)

    def step(state, parts):
        return attend_block(state, parts[0], parts[1], parts[2], parts[3])
    start = jnp.zeros((HEADS, DH, DH), jnp.float32)
    final_state, outs = lax.scan(step, start, (qs, ks, vs, ls))
    attended = outs.reshape(SEQUENCE_LENGTH, HEADS * DH)
    limit = N_CTX * N_EXP * CAP
    total = jnp.zeros((MTOK, D), jnp.float32)
    for expert in range(EXPERTS):
        chosen = route_ids == expert
        weight = lax.optimization_barrier(jnp.sum(jnp.where(chosen, route_weight, 0.0), axis=1))
        selected_routes = jnp.any(chosen, axis=1)
        index = jnp.nonzero(selected_routes, size=limit, fill_value=0)[0].astype(jnp.int32)
        valid = (jnp.arange(limit) < jnp.sum(selected_routes.astype(jnp.int32))).astype(jnp.float32)
        rows = moe_input[index]
        gate = jnp.dot(rows, gate_up[expert, :, 0, :], preferred_element_type=jnp.float32)
        upper = jnp.dot(rows, gate_up[expert, :, 1, :], preferred_element_type=jnp.float32)
        hidden = (jax.nn.silu(gate) * upper).astype(jnp.bfloat16)
        result = jnp.dot(hidden, down[expert], preferred_element_type=jnp.float32).astype(jnp.bfloat16)
        scaled = (weight[index] * valid)[:, None] * result.astype(jnp.float32)
        total = total.at[index].add(scaled)
    return (attended, total.astype(jnp.bfloat16))
```

```python
import functools

import jax
import jax.numpy as jnp
from jax import lax
from jax.experimental import pallas as pl
from jax.experimental.pallas import tpu as pltpu
from jax.sharding import PartitionSpec as P

F32, BF16 = (jnp.float32, jnp.bfloat16)
WHOLE = pl.BlockSpec(memory_space=pltpu.VMEM)
SCALARS = pl.BlockSpec(memory_space=pltpu.SMEM)
THERE = pl.BlockSpec(memory_space=pl.ANY)
MIB = 1 << 20


def prefix(shard, axis, combine, identity):
    devices, here = (lax.axis_size(axis), lax.axis_index(axis))
    everything = jax.tree.map(
        lambda part, kind: lax.all_gather(part.astype(kind), axis),
        shard,
        (jnp.bfloat16, jnp.bfloat16),
    )
    start = jax.tree.map(
        lambda part, zero: jnp.broadcast_to(jnp.asarray(zero, part.dtype), part.shape),
        shard,
        identity,
    )

    def step(k, before):
        reached = k < here
        new = combine(
            before, jax.tree.map(lambda part, own: part[k].astype(own.dtype), everything, shard)
        )
        return jax.tree.map(lambda a, b: jnp.where(reached, a, b), new, before)

    return lax.fori_loop(0, devices, step, start)


def block_terms(queries, keys, values, log_decay):
    rows = queries.shape[0]
    heads = log_decay.shape[1]
    qb = queries.reshape(rows, heads, -1)
    kb = keys.reshape(rows, heads, -1)
    vb = values.reshape(rows, heads, -1)
    cum = jnp.cumsum(log_decay, axis=0)
    diff = jnp.transpose(cum)[:, :, None] - jnp.transpose(cum)[:, None, :]
    causal = jnp.arange(rows)[:, None] >= jnp.arange(rows)[None, :]
    decay = jnp.where(causal[None, :, :], jnp.exp(jnp.minimum(diff, 0.0)), 0.0)
    scores = jnp.einsum("thd,shd->hts", qb, kb, preferred_element_type=jnp.float32)
    weights = (scores * decay).astype(jnp.bfloat16)
    intra = jnp.einsum("hts,shd->thd", weights, vb, preferred_element_type=jnp.float32)
    last = cum[-1]
    kscaled = kb.astype(jnp.float32) * jnp.exp(last[None, :] - cum)[:, :, None]
    local = jnp.einsum(
        "shd,she->hde", kscaled, vb.astype(jnp.float32), precision=lax.Precision.HIGHEST
    )
    return (qb, cum, intra, local, jnp.exp(last))


def chain_states(preceding_positions, later):
    return (
        preceding_positions[0] * later[0],
        later[0][:, None, None] * preceding_positions[1] + later[1],
    )


def route_slots(route_ids, expert_list, slots_each):
    flat_ids = route_ids.reshape(-1)
    onehot = (flat_ids[:, None] == jnp.arange(expert_list)[None, :]).astype(jnp.int32)
    slot = jnp.sum((jnp.cumsum(onehot, axis=0) - 1) * onehot, axis=1)
    target = flat_ids * slots_each + slot
    pick = jnp.arange(expert_list * slots_each)[:, None] == target[None, :]
    return (target, pick)


def on_device_any(queries, keys, values, log_decay, moe_input, route_ids, route_weight, gate_up, down):
    qb, cum, intra, local, totals = block_terms(queries, keys, values, log_decay)
    heads = log_decay.shape[1]
    width = local.shape[1]
    identity = (jnp.ones((heads,), jnp.float32), jnp.zeros((heads, width, width), jnp.float32))
    entering = prefix((totals, local), "ctx", chain_states, identity)
    qscaled = qb.astype(jnp.float32) * jnp.exp(cum)[:, :, None]
    inter = jnp.einsum("thd,hde->the", qscaled, entering[1], precision=lax.Precision.HIGHEST)
    mixed = intra + inter
    normed = mixed * lax.rsqrt(jnp.mean(mixed * mixed, axis=-1, keepdims=True) + 1e-06)
    attended = normed.astype(jnp.bfloat16).reshape(queries.shape)
    expert_list = lax.axis_size("exp")
    ctx_count = lax.axis_size("ctx")
    tok_rows = moe_input.shape[0]
    half_width = moe_input.shape[1]
    slots_each = min(tok_rows, tok_rows * 2 // expert_list + tok_rows // 4)
    target, pick = route_slots(route_ids, expert_list, slots_each)
    doubled = jnp.repeat(moe_input, 2, axis=0)
    send = jnp.dot(pick.astype(jnp.bfloat16), doubled, preferred_element_type=jnp.float32)
    send = send.astype(jnp.bfloat16).reshape(expert_list, slots_each, half_width)
    arrived = lax.all_to_all(send, "exp", split_axis=0, concat_axis=0, tiled=True)
    slot_rows = arrived.reshape(expert_list * slots_each, half_width)
    w_both = gate_up.reshape(half_width, -1)
    ff_local = w_both.shape[1] // 2
    partial_value = jnp.dot(
        lax.all_gather(slot_rows, "ctx", axis=0, tiled=True),
        w_both,
        preferred_element_type=jnp.float32,
    )
    summed = lax.psum(partial_value.astype(jnp.bfloat16), "tp").astype(jnp.float32)
    hidden = (jax.nn.silu(summed[:, :ff_local]) * summed[:, ff_local:]).astype(jnp.bfloat16)
    w_down = down.reshape(down.shape[1], down.shape[2])
    expert_out = jnp.dot(
        lax.all_gather(hidden, "ctx", axis=1, tiled=True),
        w_down,
        preferred_element_type=jnp.float32,
    ).astype(jnp.bfloat16)
    col_width = expert_out.shape[1]
    stacked = expert_out.reshape(ctx_count, expert_list, slots_each, col_width)
    back = lax.all_to_all(
        lax.all_to_all(stacked, "ctx", split_axis=0, concat_axis=3, tiled=True),
        "exp",
        split_axis=1,
        concat_axis=1,
        tiled=True,
    )
    flat = back.reshape(expert_list * slots_each, half_width)
    selected_routes = flat[target].astype(jnp.float32).reshape(tok_rows, 2, half_width)
    merged_output = jnp.sum(selected_routes * route_weight[:, :, None], axis=1)
    return (attended, merged_output.astype(jnp.bfloat16))

def cost(flops, read, transcendentals=0):
    return pl.CostEstimate(flops=flops, bytes_accessed=read, transcendentals=transcendentals)


def head_columns(h, width):
    return slice(h * width, (h + 1) * width)


def attend_kernel(heads, q_ref, k_ref, v_ref, decay_ref, weights_ref, intra_ref, local_ref, cum_ref, held_ref, sem):
    fetch = pltpu.make_async_copy(weights_ref, held_ref, sem)
    fetch.start()
    rows = q_ref.shape[0]
    width = q_ref.shape[1] // heads
    s_at = lax.broadcasted_iota(jnp.int32, (rows, rows), 0)
    t_at = lax.broadcasted_iota(jnp.int32, (rows, rows), 1)
    before = (s_at <= t_at).astype(F32)
    cum_t = jnp.dot(
        decay_ref[...], before, precision=lax.Precision.HIGHEST, preferred_element_type=F32
    )
    cum = jnp.transpose(cum_t)
    cum_ref[...] = cum
    for h in range(heads):
        at = head_columns(h, width)
        q, k, v = (q_ref[:, at], k_ref[:, at], v_ref[:, at])
        column, row = (cum[:, h : h + 1], cum_t[h : h + 1, :])
        decay = jnp.where(s_at >= t_at, jnp.exp(jnp.minimum(column - row, 0.0)), 0.0)
        scores = lax.dot_general(q, k, (((1,), (1,)), ((), ())), preferred_element_type=F32)
        intra_ref[:, at] = jnp.dot(
            (scores * decay).astype(BF16), v, preferred_element_type=F32
        )
        rest = jnp.exp(cum[rows - 1 :, h : h + 1] - column)
        scaled = (k.astype(F32) * rest).astype(BF16)
        local = lax.dot_general(scaled, v, (((0,), (0,)), ((), ())), preferred_element_type=F32)
        local_ref[h * width : (h + 1) * width, :] = local.astype(BF16)
    fetch.wait()


def attend(queries, keys, values, log_decay, gate_up):
    rows, heads = log_decay.shape
    width = queries.shape[1] // heads
    return pl.pallas_call(
        functools.partial(attend_kernel, heads),
        in_specs=[WHOLE, WHOLE, WHOLE, WHOLE, THERE],
        out_specs=[WHOLE] * 4,
        out_shape=[
            jax.ShapeDtypeStruct(queries.shape, F32),
            jax.ShapeDtypeStruct((heads * width, width), BF16),
            jax.ShapeDtypeStruct((rows, heads), F32),
            pltpu.VMEM(gate_up.shape, BF16),
        ],
        scratch_shapes=[pltpu.SemaphoreType.DMA],
        compiler_params=pltpu.CompilerParams(vmem_limit_bytes=8 * MIB),
        cost_estimate=cost(6 * rows * rows * heads * width, 2 * gate_up.size, heads * rows * rows),
        name="attend",
    )(queries, keys, values, jnp.transpose(log_decay), gate_up)


def finish_kernel(heads, q_ref, intra_ref, cum_ref, state_ref, out_ref):
    width = q_ref.shape[1] // heads
    for h in range(heads):
        at = head_columns(h, width)
        grown = jnp.exp(cum_ref[:, h : h + 1])
        state = state_ref[h * width : (h + 1) * width, :]
        mixed = intra_ref[:, at] + grown * jnp.dot(
            q_ref[:, at], state, preferred_element_type=F32
        )
        mean = jnp.mean(mixed * mixed, axis=1, keepdims=True)
        out_ref[:, at] = (mixed * lax.rsqrt(mean + 1e-06)).astype(BF16)


def finish(queries, intra, cum, state):
    rows, heads = cum.shape
    return pl.pallas_call(
        functools.partial(finish_kernel, heads),
        in_specs=[WHOLE] * 4,
        out_specs=WHOLE,
        out_shape=jax.ShapeDtypeStruct(queries.shape, BF16),
        compiler_params=pltpu.CompilerParams(vmem_limit_bytes=8 * MIB),
        cost_estimate=cost(2 * queries.size * 128, 10 * queries.size, queries.size),
        name="finish",
    )(queries, intra, cum, state)


def gate_up_kernel(x_ref, weights_ref, down_ref, sums_ref, held_ref, spread, sem):
    fetch = pltpu.make_async_copy(down_ref, held_ref, sem)
    fetch.start()
    depth, _, units = weights_ref.shape
    rows = x_ref.shape[0] * x_ref.shape[1]
    lanes = 128
    source = lax.broadcasted_iota(jnp.int32, (lanes, 2 * lanes), 0)
    goal = lax.broadcasted_iota(jnp.int32, (lanes, 2 * lanes), 1)
    even = (goal == 2 * source).astype(BF16)
    odd = (goal == 2 * source + 1).astype(BF16)
    x = x_ref[...].reshape(rows, depth)
    for b in range(depth // lanes):
        part = x[:, b * lanes : (b + 1) * lanes]
        to = slice(2 * b * lanes, 2 * (b + 1) * lanes)
        spread[:rows, to] = jnp.dot(part, even, preferred_element_type=F32).astype(BF16)
        spread[rows:, to] = jnp.dot(part, odd, preferred_element_type=F32).astype(BF16)
    step = 768
    total = jnp.zeros((2 * rows, units), F32)
    for start in range(0, depth, step):
        weights = weights_ref[start : start + step].reshape(2 * step, units)
        total += jnp.dot(
            spread[:, 2 * start : 2 * (start + step)], weights, preferred_element_type=F32
        )
    sums_ref[...] = total.astype(BF16)
    fetch.wait()


def gate_up_sums(x, weights, down):
    rows = x.shape[0] * x.shape[1]
    depth, _, units = weights.shape
    return pl.pallas_call(
        gate_up_kernel,
        in_specs=[WHOLE, WHOLE, THERE],
        out_specs=[WHOLE, WHOLE],
        out_shape=[
            jax.ShapeDtypeStruct((2 * rows, units), BF16),
            pltpu.VMEM(down.shape, BF16),
        ],
        scratch_shapes=[pltpu.VMEM((2 * rows, 2 * depth), BF16), pltpu.SemaphoreType.DMA],
        compiler_params=pltpu.CompilerParams(vmem_limit_bytes=8 * MIB),
        cost_estimate=cost(4 * rows * weights.size, 2 * weights.size),
        name="gate_up_sums",
    )(x, pltpu.with_memory_space_constraint(weights, pltpu.VMEM), down)


def hidden_kernel(own_ref, other_ref, out_ref):
    rows = out_ref.shape[0]
    summed = own_ref[...].astype(F32) + other_ref[...].astype(F32)
    gate, up = (summed[:rows], summed[rows:])
    out_ref[...] = (gate / (1.0 + jnp.exp(-gate)) * up).astype(BF16)


def hidden_units(own, other):
    rows, units = own.shape
    return pl.pallas_call(
        hidden_kernel,
        in_specs=[WHOLE] * 2,
        out_specs=WHOLE,
        out_shape=jax.ShapeDtypeStruct((rows // 2, units), BF16),
        compiler_params=pltpu.CompilerParams(vmem_limit_bytes=8 * MIB),
        cost_estimate=cost(4 * own.size, 5 * own.size, own.size // 2),
        name="hidden_units",
    )(own, other)


def down_own_kernel(here_ref, hidden_ref, down_ref, out_ref):
    units = hidden_ref.shape[1]
    first = pl.multiple_of(here_ref[0] * units, units)
    out_ref[...] = jnp.dot(
        hidden_ref[...], down_ref[pl.ds(first, units), :], preferred_element_type=F32
    )


def down_other_kernel(here_ref, hidden_ref, down_ref, own_ref, out_ref):
    units = hidden_ref.shape[1]
    first = pl.multiple_of(here_ref[0] * units, units)
    total = own_ref[...] + jnp.dot(
        hidden_ref[...], down_ref[pl.ds(first, units), :], preferred_element_type=F32
    )
    out_ref[...] = total.astype(BF16).reshape(out_ref.shape)


def down_sums(place, hidden, down, own=None, peers=None):
    rows, units = hidden.shape
    columns = down.shape[1]
    place = place.astype(jnp.int32).reshape(1)
    down = pltpu.with_memory_space_constraint(down, pltpu.VMEM)
    if own is None:
        kernel, operands = (down_own_kernel, (place, hidden, down))
        out_shape = jax.ShapeDtypeStruct((rows, columns), F32)
    else:
        kernel, operands = (down_other_kernel, (place, hidden, down, own))
        out_shape = jax.ShapeDtypeStruct((peers, rows // peers, columns), BF16)
    return pl.pallas_call(
        kernel,
        in_specs=[SCALARS] + [WHOLE] * (len(operands) - 1),
        out_specs=WHOLE,
        out_shape=out_shape,
        compiler_params=pltpu.CompilerParams(vmem_limit_bytes=8 * MIB),
        cost_estimate=cost(2 * rows * units * columns, 2 * units * columns),
        name="down_own" if own is None else "down_other",
    )(*operands)


def merge_kernel(ids_ref, weight_ref, back_ref, out_ref):
    ctx_count, _, rows, columns = back_ref.shape
    for i in range(rows):
        for c in range(ctx_count):
            picked = [
                back_ref[c, ids_ref[k, i], i : i + 1, :].astype(F32) * weight_ref[k, i]
                for k in range(2)
            ]
            out_ref[i : i + 1, c * columns : (c + 1) * columns] = (picked[0] + picked[1]).astype(BF16)


def merge(route_ids, route_weight, back):
    ctx_count, _, rows, columns = back.shape
    return pl.pallas_call(
        merge_kernel,
        in_specs=[SCALARS, SCALARS, WHOLE],
        out_specs=WHOLE,
        out_shape=jax.ShapeDtypeStruct((rows, ctx_count * columns), BF16),
        compiler_params=pltpu.CompilerParams(vmem_limit_bytes=8 * MIB),
        cost_estimate=cost(4 * back.size, 2 * back.size),
        name="merge",
    )(jnp.transpose(route_ids), jnp.transpose(route_weight), back)


def on_device(queries, keys, values, log_decay, moe_input, route_ids, route_weight, gate_up, down):
    ctx_count, expert_list = (lax.axis_size("ctx"), lax.axis_size("exp"))
    if ctx_count != 2 or lax.axis_size("tp") != 2 or gate_up.shape[3] % 128:
        return on_device_any(
            queries, keys, values, log_decay, moe_input, route_ids, route_weight, gate_up, down
        )
    here = lax.axis_index("ctx")
    peers = ctx_count * expert_list
    swap = [(0, 1), (1, 0)]
    tokens = lax.all_to_all(
        jnp.broadcast_to(moe_input[None], (peers,) + moe_input.shape),
        ("ctx", "exp"),
        split_axis=0,
        concat_axis=0,
        tiled=True,
    )
    intra, local, cum, weights = attend(
        queries, keys, values, log_decay, gate_up.reshape(gate_up.shape[1:])
    )
    state = lax.ppermute(local, "ctx", [(0, 1)])
    sums, w_down = gate_up_sums(tokens, weights, down.reshape(down.shape[1:]))
    hidden = hidden_units(sums, lax.ppermute(sums, "tp", swap))
    hidden_other = lax.ppermute(hidden, "ctx", swap)
    own = down_sums(here, hidden, w_down)
    expert_out = down_sums(1 - here, hidden_other, w_down, own, peers)
    back = lax.all_to_all(expert_out, ("ctx", "exp"), split_axis=0, concat_axis=0, tiled=True)
    attended = finish(queries, intra, cum, state)
    back = back.reshape((ctx_count, expert_list) + back.shape[1:])
    return (attended, merge(route_ids, route_weight, back))


def solution(mesh):
    in_specs = (
        P(("groups", "ctx"), ("exp", "tp")),
        P(("groups", "ctx"), ("exp", "tp")),
        P(("groups", "ctx"), ("exp", "tp")),
        P(("groups", "ctx"), ("exp", "tp")),
        P(("groups", "ctx", "exp"), "tp"),
        P(("groups", "ctx", "exp"), None),
        P(("groups", "ctx", "exp"), None),
        P("exp", "tp", None, "ctx"),
        P("exp", None, ("tp", "ctx")),
    )
    out_specs = (P(("groups", "ctx"), ("exp", "tp")), P(("groups", "ctx", "exp"), "tp"))
    return jax.shard_map(
        on_device, mesh=mesh, in_specs=in_specs, out_specs=out_specs, check_vma=False
    )
```

```python
import functools

import jax
import jax.numpy as jnp
from jax import lax
from jax.experimental import pallas as pl
from jax.experimental.pallas import tpu as pltpu
from jax.sharding import PartitionSpec as P

F32, BF16 = (jnp.float32, jnp.bfloat16)
WHOLE = pl.BlockSpec(memory_space=pltpu.VMEM)
SCALARS = pl.BlockSpec(memory_space=pltpu.SMEM)
THERE = pl.BlockSpec(memory_space=pl.ANY)
MIB = 1 << 20


def prefix(shard, axis, combine, identity):
    devices, here = (lax.axis_size(axis), lax.axis_index(axis))
    everything = jax.tree.map(
        lambda part, kind: lax.all_gather(part.astype(kind), axis),
        shard,
        (jnp.bfloat16, jnp.bfloat16),
    )
    start = jax.tree.map(
        lambda part, zero: jnp.broadcast_to(jnp.asarray(zero, part.dtype), part.shape),
        shard,
        identity,
    )

    def step(k, before):
        reached = k < here
        new = combine(
            before, jax.tree.map(lambda part, own: part[k].astype(own.dtype), everything, shard)
        )
        return jax.tree.map(lambda a, b: jnp.where(reached, a, b), new, before)

    return lax.fori_loop(0, devices, step, start)


def block_terms(queries, keys, values, log_decay):
    rows = queries.shape[0]
    heads = log_decay.shape[1]
    qb = queries.reshape(rows, heads, -1)
    kb = keys.reshape(rows, heads, -1)
    vb = values.reshape(rows, heads, -1)
    cum = jnp.cumsum(log_decay, axis=0)
    diff = jnp.transpose(cum)[:, :, None] - jnp.transpose(cum)[:, None, :]
    causal = jnp.arange(rows)[:, None] >= jnp.arange(rows)[None, :]
    decay = jnp.where(causal[None, :, :], jnp.exp(jnp.minimum(diff, 0.0)), 0.0)
    scores = jnp.einsum("thd,shd->hts", qb, kb, preferred_element_type=jnp.float32)
    weights = (scores * decay).astype(jnp.bfloat16)
    intra = jnp.einsum("hts,shd->thd", weights, vb, preferred_element_type=jnp.float32)
    last = cum[-1]
    kscaled = kb.astype(jnp.float32) * jnp.exp(last[None, :] - cum)[:, :, None]
    local = jnp.einsum(
        "shd,she->hde", kscaled, vb.astype(jnp.float32), precision=lax.Precision.HIGHEST
    )
    return (qb, cum, intra, local, jnp.exp(last))


def chain_states(preceding_positions, later):
    return (
        preceding_positions[0] * later[0],
        later[0][:, None, None] * preceding_positions[1] + later[1],
    )


def route_slots(route_ids, expert_list, slots_each):
    flat_ids = route_ids.reshape(-1)
    onehot = (flat_ids[:, None] == jnp.arange(expert_list)[None, :]).astype(jnp.int32)
    slot = jnp.sum((jnp.cumsum(onehot, axis=0) - 1) * onehot, axis=1)
    target = flat_ids * slots_each + slot
    pick = jnp.arange(expert_list * slots_each)[:, None] == target[None, :]
    return (target, pick)


def on_device_any(queries, keys, values, log_decay, moe_input, route_ids, route_weight, gate_up, down):
    qb, cum, intra, local, totals = block_terms(queries, keys, values, log_decay)
    heads = log_decay.shape[1]
    width = local.shape[1]
    identity = (jnp.ones((heads,), jnp.float32), jnp.zeros((heads, width, width), jnp.float32))
    entering = prefix((totals, local), "ctx", chain_states, identity)
    qscaled = qb.astype(jnp.float32) * jnp.exp(cum)[:, :, None]
    inter = jnp.einsum("thd,hde->the", qscaled, entering[1], precision=lax.Precision.HIGHEST)
    mixed = intra + inter
    normed = mixed * lax.rsqrt(jnp.mean(mixed * mixed, axis=-1, keepdims=True) + 1e-06)
    attended = normed.astype(jnp.bfloat16).reshape(queries.shape)
    expert_list = lax.axis_size("exp")
    ctx_count = lax.axis_size("ctx")
    tok_rows = moe_input.shape[0]
    half_width = moe_input.shape[1]
    slots_each = min(tok_rows, tok_rows * 2 // expert_list + tok_rows // 4)
    target, pick = route_slots(route_ids, expert_list, slots_each)
    doubled = jnp.repeat(moe_input, 2, axis=0)
    send = jnp.dot(pick.astype(jnp.bfloat16), doubled, preferred_element_type=jnp.float32)
    send = send.astype(jnp.bfloat16).reshape(expert_list, slots_each, half_width)
    arrived = lax.all_to_all(send, "exp", split_axis=0, concat_axis=0, tiled=True)
    slot_rows = arrived.reshape(expert_list * slots_each, half_width)
    w_both = gate_up.reshape(half_width, -1)
    ff_local = w_both.shape[1] // 2
    partial_value = jnp.dot(
        lax.all_gather(slot_rows, "ctx", axis=0, tiled=True),
        w_both,
        preferred_element_type=jnp.float32,
    )
    summed = lax.psum(partial_value.astype(jnp.bfloat16), "tp").astype(jnp.float32)
    hidden = (jax.nn.silu(summed[:, :ff_local]) * summed[:, ff_local:]).astype(jnp.bfloat16)
    w_down = down.reshape(down.shape[1], down.shape[2])
    expert_out = jnp.dot(
        lax.all_gather(hidden, "ctx", axis=1, tiled=True),
        w_down,
        preferred_element_type=jnp.float32,
    ).astype(jnp.bfloat16)
    col_width = expert_out.shape[1]
    stacked = expert_out.reshape(ctx_count, expert_list, slots_each, col_width)
    back = lax.all_to_all(
        lax.all_to_all(stacked, "ctx", split_axis=0, concat_axis=3, tiled=True),
        "exp",
        split_axis=1,
        concat_axis=1,
        tiled=True,
    )
    flat = back.reshape(expert_list * slots_each, half_width)
    selected_routes = flat[target].astype(jnp.float32).reshape(tok_rows, 2, half_width)
    merged_output = jnp.sum(selected_routes * route_weight[:, :, None], axis=1)
    return (attended, merged_output.astype(jnp.bfloat16))

def cost(flops, read, transcendentals=0):
    return pl.CostEstimate(flops=flops, bytes_accessed=read, transcendentals=transcendentals)


def head_columns(h, width):
    return slice(h * width, (h + 1) * width)


def attend_kernel(heads, q_hbm, k_hbm, v_hbm, decay_hbm, intra_ref, local_ref, cum_ref, q_ref, k_ref, v_ref, decay_ref, sems):
    pairs = ((decay_hbm, decay_ref), (q_hbm, q_ref), (k_hbm, k_ref), (v_hbm, v_ref))
    fetches = [pltpu.make_async_copy(a, b, sems.at[i]) for i, (a, b) in enumerate(pairs)]
    for fetch in fetches:
        fetch.start()
    rows = q_ref.shape[0]
    width = q_ref.shape[1] // heads
    s_at = lax.broadcasted_iota(jnp.int32, (rows, rows), 0)
    t_at = lax.broadcasted_iota(jnp.int32, (rows, rows), 1)
    before = (s_at <= t_at).astype(F32)
    fetches[0].wait()
    cum_t = jnp.dot(
        decay_ref[...], before, precision=lax.Precision.HIGHEST, preferred_element_type=F32
    )
    cum = jnp.transpose(cum_t)
    cum_ref[...] = cum
    for fetch in fetches[1:]:
        fetch.wait()
    for h in range(heads):
        at = head_columns(h, width)
        q, k, v = (q_ref[:, at], k_ref[:, at], v_ref[:, at])
        column, row = (cum[:, h : h + 1], cum_t[h : h + 1, :])
        decay = jnp.where(s_at >= t_at, jnp.exp(jnp.minimum(column - row, 0.0)), 0.0)
        scores = lax.dot_general(q, k, (((1,), (1,)), ((), ())), preferred_element_type=F32)
        intra_ref[:, at] = jnp.dot(
            (scores * decay).astype(BF16), v, preferred_element_type=F32
        )
        rest = jnp.exp(cum[rows - 1 :, h : h + 1] - column)
        scaled = (k.astype(F32) * rest).astype(BF16)
        local = lax.dot_general(scaled, v, (((0,), (0,)), ((), ())), preferred_element_type=F32)
        local_ref[h * width : (h + 1) * width, :] = local.astype(BF16)


def attend(queries, keys, values, log_decay):
    rows, heads = log_decay.shape
    width = queries.shape[1] // heads
    return pl.pallas_call(
        functools.partial(attend_kernel, heads),
        in_specs=[THERE] * 4,
        out_specs=[WHOLE] * 3,
        out_shape=[
            jax.ShapeDtypeStruct(queries.shape, F32),
            jax.ShapeDtypeStruct((heads * width, width), BF16),
            jax.ShapeDtypeStruct((rows, heads), F32),
        ],
        scratch_shapes=[pltpu.VMEM(queries.shape, BF16)] * 3
        + [pltpu.VMEM((heads, rows), F32), pltpu.SemaphoreType.DMA((4,))],
        compiler_params=pltpu.CompilerParams(vmem_limit_bytes=8 * MIB),
        cost_estimate=cost(6 * rows * rows * heads * width, 6 * queries.size, heads * rows * rows),
        name="attend",
    )(queries, keys, values, jnp.transpose(log_decay))


def finish_kernel(heads, q_ref, intra_ref, cum_ref, state_ref, out_ref):
    width = q_ref.shape[1] // heads
    for h in range(heads):
        at = head_columns(h, width)
        grown = jnp.exp(cum_ref[:, h : h + 1])
        state = state_ref[h * width : (h + 1) * width, :]
        mixed = intra_ref[:, at] + grown * jnp.dot(
            q_ref[:, at], state, preferred_element_type=F32
        )
        mean = jnp.mean(mixed * mixed, axis=1, keepdims=True)
        out_ref[:, at] = (mixed * lax.rsqrt(mean + 1e-06)).astype(BF16)


def finish(queries, intra, cum, state):
    rows, heads = cum.shape
    return pl.pallas_call(
        functools.partial(finish_kernel, heads),
        in_specs=[WHOLE] * 4,
        out_specs=WHOLE,
        out_shape=jax.ShapeDtypeStruct(queries.shape, BF16),
        compiler_params=pltpu.CompilerParams(vmem_limit_bytes=8 * MIB),
        cost_estimate=cost(2 * queries.size * 128, 10 * queries.size, queries.size),
        name="finish",
    )(queries, intra, cum, state)


def gate_up_kernel(step, x_ref, weights_hbm, sums_ref, weights_ref, spread, sems):
    depth, _, units = weights_ref.shape
    starts = range(0, depth, step)
    fetches = [
        pltpu.make_async_copy(
            weights_hbm.at[pl.ds(start, step)], weights_ref.at[pl.ds(start, step)], sems.at[i]
        )
        for i, start in enumerate(starts)
    ]
    for fetch in fetches:
        fetch.start()
    rows = x_ref.shape[0] * x_ref.shape[1]
    lanes = 128
    source = lax.broadcasted_iota(jnp.int32, (lanes, 2 * lanes), 0)
    goal = lax.broadcasted_iota(jnp.int32, (lanes, 2 * lanes), 1)
    even = (goal == 2 * source).astype(BF16)
    odd = (goal == 2 * source + 1).astype(BF16)
    x = x_ref[...].reshape(rows, depth)
    for b in range(depth // lanes):
        part = x[:, b * lanes : (b + 1) * lanes]
        to = slice(2 * b * lanes, 2 * (b + 1) * lanes)
        spread[:rows, to] = jnp.dot(part, even, preferred_element_type=F32).astype(BF16)
        spread[rows:, to] = jnp.dot(part, odd, preferred_element_type=F32).astype(BF16)
    total = jnp.zeros((2 * rows, units), F32)
    for start, fetch in zip(starts, fetches):
        fetch.wait()
        weights = weights_ref[start : start + step].reshape(2 * step, units)
        total += jnp.dot(
            spread[:, 2 * start : 2 * (start + step)], weights, preferred_element_type=F32
        )
    sums_ref[...] = total.astype(BF16)


def gate_up_sums(x, weights):
    rows = x.shape[0] * x.shape[1]
    depth, _, units = weights.shape
    step = 384
    return pl.pallas_call(
        functools.partial(gate_up_kernel, step),
        in_specs=[WHOLE, THERE],
        out_specs=WHOLE,
        out_shape=jax.ShapeDtypeStruct((2 * rows, units), BF16),
        scratch_shapes=[
            pltpu.VMEM(weights.shape, BF16),
            pltpu.VMEM((2 * rows, 2 * depth), BF16),
            pltpu.SemaphoreType.DMA((depth // step,)),
        ],
        compiler_params=pltpu.CompilerParams(vmem_limit_bytes=36 * MIB),
        cost_estimate=cost(4 * rows * weights.size, 2 * weights.size),
        name="gate_up_sums",
    )(x, weights)


def hidden_kernel(own_ref, other_ref, out_ref):
    rows = out_ref.shape[0]
    summed = own_ref[...].astype(F32) + other_ref[...].astype(F32)
    gate, up = (summed[:rows], summed[rows:])
    out_ref[...] = (gate / (1.0 + jnp.exp(-gate)) * up).astype(BF16)


def hidden_units(own, other):
    rows, units = own.shape
    return pl.pallas_call(
        hidden_kernel,
        in_specs=[WHOLE] * 2,
        out_specs=WHOLE,
        out_shape=jax.ShapeDtypeStruct((rows // 2, units), BF16),
        compiler_params=pltpu.CompilerParams(vmem_limit_bytes=8 * MIB),
        cost_estimate=cost(4 * own.size, 5 * own.size, own.size // 2),
        name="hidden_units",
    )(own, other)


def down_own_kernel(hidden_ref, down_ref, out_ref):
    units = hidden_ref.shape[1]
    first = pl.multiple_of(lax.axis_index("ctx") * units, units)
    out_ref[...] = jnp.dot(
        hidden_ref[...], down_ref[pl.ds(first, units), :], preferred_element_type=F32
    )


def down_other_kernel(hidden_ref, down_ref, own_ref, out_ref):
    units = hidden_ref.shape[1]
    first = pl.multiple_of((1 - lax.axis_index("ctx")) * units, units)
    total = own_ref[...] + jnp.dot(
        hidden_ref[...], down_ref[pl.ds(first, units), :], preferred_element_type=F32
    )
    out_ref[...] = total.astype(BF16).reshape(out_ref.shape)


def down_sums(hidden, down, own=None, peers=None):
    rows, units = hidden.shape
    columns = down.shape[1]
    down = pltpu.with_memory_space_constraint(down, pltpu.VMEM)
    if own is None:
        kernel, operands = (down_own_kernel, (hidden, down))
        out_shape = jax.ShapeDtypeStruct((rows, columns), F32)
    else:
        kernel, operands = (down_other_kernel, (hidden, down, own))
        out_shape = jax.ShapeDtypeStruct((peers, rows // peers, columns), BF16)
    return pl.pallas_call(
        kernel,
        in_specs=[WHOLE] * len(operands),
        out_specs=WHOLE,
        out_shape=out_shape,
        compiler_params=pltpu.CompilerParams(vmem_limit_bytes=8 * MIB),
        cost_estimate=cost(2 * rows * units * columns, 2 * units * columns),
        name="down_own" if own is None else "down_other",
    )(*operands)


def merge_kernel(ids_ref, weight_ref, back_ref, out_ref, table):
    ctx_count, experts, rows, columns = back_ref.shape
    ids, weight = (ids_ref[...], weight_ref[...])
    for e in range(experts):
        table[e : e + 1, :rows] = jnp.sum(
            jnp.where(ids == e, weight, 0.0), axis=0, keepdims=True
        )
    share = jnp.transpose(table[...])
    for c in range(ctx_count):
        total = jnp.zeros((rows, columns), F32)
        for e in range(experts):
            total += share[:rows, e : e + 1] * back_ref[c, e].astype(F32)
        out_ref[:, c * columns : (c + 1) * columns] = total.astype(BF16)


def merge(route_ids, route_weight, back):
    ctx_count, experts, rows, columns = back.shape
    return pl.pallas_call(
        merge_kernel,
        in_specs=[WHOLE] * 3,
        out_specs=WHOLE,
        out_shape=jax.ShapeDtypeStruct((rows, ctx_count * columns), BF16),
        scratch_shapes=[pltpu.VMEM((8, 128), F32)],
        compiler_params=pltpu.CompilerParams(vmem_limit_bytes=8 * MIB),
        cost_estimate=cost(4 * back.size, 2 * back.size),
        name="merge",
    )(jnp.transpose(route_ids), jnp.transpose(route_weight), back)


def on_device(queries, keys, values, log_decay, moe_input, route_ids, route_weight, gate_up, down):
    ctx_count, expert_list = (lax.axis_size("ctx"), lax.axis_size("exp"))
    if ctx_count != 2 or lax.axis_size("tp") != 2 or gate_up.shape[3] % 128:
        return on_device_any(
            queries, keys, values, log_decay, moe_input, route_ids, route_weight, gate_up, down
        )
    peers = ctx_count * expert_list
    swap = [(0, 1), (1, 0)]
    tokens = lax.all_to_all(
        jnp.broadcast_to(moe_input[None], (peers,) + moe_input.shape),
        ("ctx", "exp"),
        split_axis=0,
        concat_axis=0,
        tiled=True,
    )
    intra, local, cum = attend(queries, keys, values, log_decay)
    state = lax.ppermute(local, "ctx", [(0, 1)])
    sums = gate_up_sums(tokens, gate_up.reshape(gate_up.shape[1:]))
    sums, w_down = lax.optimization_barrier((sums, down.reshape(down.shape[1:])))
    hidden = hidden_units(sums, lax.ppermute(sums, "tp", swap))
    hidden_other = lax.ppermute(hidden, "ctx", swap)
    own = down_sums(hidden, w_down)
    expert_out = down_sums(hidden_other, w_down, own, peers)
    back = lax.all_to_all(expert_out, ("ctx", "exp"), split_axis=0, concat_axis=0, tiled=True)
    attended = finish(queries, intra, cum, state)
    back = back.reshape((ctx_count, expert_list) + back.shape[1:])
    return (attended, merge(route_ids, route_weight, back))


def solution(mesh):
    in_specs = (
        P(("groups", "ctx"), ("exp", "tp")),
        P(("groups", "ctx"), ("exp", "tp")),
        P(("groups", "ctx"), ("exp", "tp")),
        P(("groups", "ctx"), ("exp", "tp")),
        P(("groups", "ctx", "exp"), "tp"),
        P(("groups", "ctx", "exp"), None),
        P(("groups", "ctx", "exp"), None),
        P("exp", "tp", None, "ctx"),
        P("exp", None, ("tp", "ctx")),
    )
    out_specs = (P(("groups", "ctx"), ("exp", "tp")), P(("groups", "ctx", "exp"), "tp"))
    return jax.shard_map(
        on_device, mesh=mesh, in_specs=in_specs, out_specs=out_specs, check_vma=False
    )
```

```python
import functools

import jax
import jax.numpy as jnp
from jax import lax
from jax.experimental import pallas as pl
from jax.experimental.pallas import tpu as pltpu
from jax.sharding import PartitionSpec as P

F32, BF16 = (jnp.float32, jnp.bfloat16)
WHOLE = pl.BlockSpec(memory_space=pltpu.VMEM)
SCALARS = pl.BlockSpec(memory_space=pltpu.SMEM)
THERE = pl.BlockSpec(memory_space=pl.ANY)
MIB = 1 << 20


def prefix(shard, axis, combine, identity):
    devices, here = (lax.axis_size(axis), lax.axis_index(axis))
    everything = jax.tree.map(
        lambda part, kind: lax.all_gather(part.astype(kind), axis),
        shard,
        (jnp.bfloat16, jnp.bfloat16),
    )
    start = jax.tree.map(
        lambda part, zero: jnp.broadcast_to(jnp.asarray(zero, part.dtype), part.shape),
        shard,
        identity,
    )

    def step(k, before):
        reached = k < here
        new = combine(
            before, jax.tree.map(lambda part, own: part[k].astype(own.dtype), everything, shard)
        )
        return jax.tree.map(lambda a, b: jnp.where(reached, a, b), new, before)

    return lax.fori_loop(0, devices, step, start)


def block_terms(queries, keys, values, log_decay):
    rows = queries.shape[0]
    heads = log_decay.shape[1]
    qb = queries.reshape(rows, heads, -1)
    kb = keys.reshape(rows, heads, -1)
    vb = values.reshape(rows, heads, -1)
    cum = jnp.cumsum(log_decay, axis=0)
    diff = jnp.transpose(cum)[:, :, None] - jnp.transpose(cum)[:, None, :]
    causal = jnp.arange(rows)[:, None] >= jnp.arange(rows)[None, :]
    decay = jnp.where(causal[None, :, :], jnp.exp(jnp.minimum(diff, 0.0)), 0.0)
    scores = jnp.einsum("thd,shd->hts", qb, kb, preferred_element_type=jnp.float32)
    weights = (scores * decay).astype(jnp.bfloat16)
    intra = jnp.einsum("hts,shd->thd", weights, vb, preferred_element_type=jnp.float32)
    last = cum[-1]
    kscaled = kb.astype(jnp.float32) * jnp.exp(last[None, :] - cum)[:, :, None]
    local = jnp.einsum(
        "shd,she->hde", kscaled, vb.astype(jnp.float32), precision=lax.Precision.HIGHEST
    )
    return (qb, cum, intra, local, jnp.exp(last))


def chain_states(preceding_positions, later):
    return (
        preceding_positions[0] * later[0],
        later[0][:, None, None] * preceding_positions[1] + later[1],
    )


def route_slots(route_ids, expert_list, slots_each):
    flat_ids = route_ids.reshape(-1)
    onehot = (flat_ids[:, None] == jnp.arange(expert_list)[None, :]).astype(jnp.int32)
    slot = jnp.sum((jnp.cumsum(onehot, axis=0) - 1) * onehot, axis=1)
    target = flat_ids * slots_each + slot
    pick = jnp.arange(expert_list * slots_each)[:, None] == target[None, :]
    return (target, pick)


def on_device_any(queries, keys, values, log_decay, moe_input, route_ids, route_weight, gate_up, down):
    qb, cum, intra, local, totals = block_terms(queries, keys, values, log_decay)
    heads = log_decay.shape[1]
    width = local.shape[1]
    identity = (jnp.ones((heads,), jnp.float32), jnp.zeros((heads, width, width), jnp.float32))
    entering = prefix((totals, local), "ctx", chain_states, identity)
    qscaled = qb.astype(jnp.float32) * jnp.exp(cum)[:, :, None]
    inter = jnp.einsum("thd,hde->the", qscaled, entering[1], precision=lax.Precision.HIGHEST)
    mixed = intra + inter
    normed = mixed * lax.rsqrt(jnp.mean(mixed * mixed, axis=-1, keepdims=True) + 1e-06)
    attended = normed.astype(jnp.bfloat16).reshape(queries.shape)
    expert_list = lax.axis_size("exp")
    ctx_count = lax.axis_size("ctx")
    tok_rows = moe_input.shape[0]
    half_width = moe_input.shape[1]
    slots_each = min(tok_rows, tok_rows * 2 // expert_list + tok_rows // 4)
    target, pick = route_slots(route_ids, expert_list, slots_each)
    doubled = jnp.repeat(moe_input, 2, axis=0)
    send = jnp.dot(pick.astype(jnp.bfloat16), doubled, preferred_element_type=jnp.float32)
    send = send.astype(jnp.bfloat16).reshape(expert_list, slots_each, half_width)
    arrived = lax.all_to_all(send, "exp", split_axis=0, concat_axis=0, tiled=True)
    slot_rows = arrived.reshape(expert_list * slots_each, half_width)
    w_both = gate_up.reshape(half_width, -1)
    ff_local = w_both.shape[1] // 2
    partial_value = jnp.dot(
        lax.all_gather(slot_rows, "ctx", axis=0, tiled=True),
        w_both,
        preferred_element_type=jnp.float32,
    )
    summed = lax.psum(partial_value.astype(jnp.bfloat16), "tp").astype(jnp.float32)
    hidden = (jax.nn.silu(summed[:, :ff_local]) * summed[:, ff_local:]).astype(jnp.bfloat16)
    w_down = down.reshape(down.shape[1], down.shape[2])
    expert_out = jnp.dot(
        lax.all_gather(hidden, "ctx", axis=1, tiled=True),
        w_down,
        preferred_element_type=jnp.float32,
    ).astype(jnp.bfloat16)
    col_width = expert_out.shape[1]
    stacked = expert_out.reshape(ctx_count, expert_list, slots_each, col_width)
    back = lax.all_to_all(
        lax.all_to_all(stacked, "ctx", split_axis=0, concat_axis=3, tiled=True),
        "exp",
        split_axis=1,
        concat_axis=1,
        tiled=True,
    )
    flat = back.reshape(expert_list * slots_each, half_width)
    selected_routes = flat[target].astype(jnp.float32).reshape(tok_rows, 2, half_width)
    merged_output = jnp.sum(selected_routes * route_weight[:, :, None], axis=1)
    return (attended, merged_output.astype(jnp.bfloat16))

def cost(flops, read, transcendentals=0):
    return pl.CostEstimate(flops=flops, bytes_accessed=read, transcendentals=transcendentals)


def head_columns(h, width):
    return slice(h * width, (h + 1) * width)


def attend_kernel(
    heads, q_hbm, k_hbm, v_hbm, decay_hbm, weights_hbm, intra_ref, local_ref, cum_ref, held_ref,
    q_ref, k_ref, v_ref, decay_ref, sems,
):
    pairs = (
        (decay_hbm, decay_ref),
        (q_hbm, q_ref),
        (k_hbm, k_ref),
        (v_hbm, v_ref),
        (weights_hbm.at[pl.ds(0, held_ref.shape[0])], held_ref),
    )
    fetches = [pltpu.make_async_copy(a, b, sems.at[i]) for i, (a, b) in enumerate(pairs)]
    for fetch in fetches:
        fetch.start()
    rows = q_ref.shape[0]
    width = q_ref.shape[1] // heads
    s_at = lax.broadcasted_iota(jnp.int32, (rows, rows), 0)
    t_at = lax.broadcasted_iota(jnp.int32, (rows, rows), 1)
    before = (s_at <= t_at).astype(F32)
    fetches[0].wait()
    cum_t = jnp.dot(
        decay_ref[...], before, precision=lax.Precision.HIGHEST, preferred_element_type=F32
    )
    cum = jnp.transpose(cum_t)
    cum_ref[...] = cum
    for fetch in fetches[1:4]:
        fetch.wait()
    for h in range(heads):
        at = head_columns(h, width)
        q, k, v = (q_ref[:, at], k_ref[:, at], v_ref[:, at])
        column, row = (cum[:, h : h + 1], cum_t[h : h + 1, :])
        decay = jnp.where(s_at >= t_at, jnp.exp(jnp.minimum(column - row, 0.0)), 0.0)
        scores = lax.dot_general(q, k, (((1,), (1,)), ((), ())), preferred_element_type=F32)
        intra_ref[:, at] = jnp.dot(
            (scores * decay).astype(BF16), v, preferred_element_type=F32
        )
        rest = jnp.exp(cum[rows - 1 :, h : h + 1] - column)
        scaled = (k.astype(F32) * rest).astype(BF16)
        local = lax.dot_general(scaled, v, (((0,), (0,)), ((), ())), preferred_element_type=F32)
        local_ref[h * width : (h + 1) * width, :] = local.astype(BF16)
    fetches[4].wait()


def attend(queries, keys, values, log_decay, weights, depth):
    rows, heads = log_decay.shape
    width = queries.shape[1] // heads
    operands = (queries, keys, values, jnp.transpose(log_decay), weights)
    return pl.pallas_call(
        functools.partial(attend_kernel, heads),
        in_specs=[THERE] * 5,
        out_specs=[WHOLE] * 4,
        out_shape=[
            jax.ShapeDtypeStruct(queries.shape, F32),
            jax.ShapeDtypeStruct((heads * width, width), BF16),
            jax.ShapeDtypeStruct((rows, heads), F32),
            pltpu.VMEM((depth,) + weights.shape[1:], BF16),
        ],
        scratch_shapes=[pltpu.VMEM(queries.shape, BF16)] * 3
        + [pltpu.VMEM((heads, rows), F32), pltpu.SemaphoreType.DMA((5,))],
        compiler_params=pltpu.CompilerParams(vmem_limit_bytes=8 * MIB),
        cost_estimate=cost(10**10, 6 * queries.size, heads * rows * rows),
        name="attend",
    )(*(pltpu.with_memory_space_constraint(x, pltpu.HBM) for x in operands))


def finish_kernel(heads, q_ref, intra_ref, cum_ref, state_ref, out_ref):
    width = q_ref.shape[1] // heads
    for h in range(heads):
        at = head_columns(h, width)
        grown = jnp.exp(cum_ref[:, h : h + 1])
        state = state_ref[h * width : (h + 1) * width, :]
        mixed = intra_ref[:, at] + grown * jnp.dot(
            q_ref[:, at], state, preferred_element_type=F32
        )
        mean = jnp.mean(mixed * mixed, axis=1, keepdims=True)
        out_ref[:, at] = (mixed * lax.rsqrt(mean + 1e-06)).astype(BF16)


def finish(queries, intra, cum, state):
    rows, heads = cum.shape
    return pl.pallas_call(
        functools.partial(finish_kernel, heads),
        in_specs=[WHOLE] * 4,
        out_specs=WHOLE,
        out_shape=jax.ShapeDtypeStruct(queries.shape, BF16),
        compiler_params=pltpu.CompilerParams(vmem_limit_bytes=8 * MIB),
        cost_estimate=cost(2 * queries.size * 128, 10 * queries.size, queries.size),
        name="finish",
    )(queries, intra, cum, state)


def join_kernel(first_ref, second_ref, out_ref):
    count = first_ref.shape[0]
    out_ref[:count] = first_ref[...]
    out_ref[count:] = second_ref[...]


def join(first, second):
    return pl.pallas_call(
        join_kernel,
        in_specs=[WHOLE] * 2,
        out_specs=WHOLE,
        out_shape=jax.ShapeDtypeStruct((2 * first.shape[0],) + first.shape[1:], first.dtype),
        compiler_params=pltpu.CompilerParams(vmem_limit_bytes=4 * MIB),
        cost_estimate=cost(3 * 10**9, 8 * first.size),
        name="join",
    )(first, second)


def hold_kernel(first, after_ref, weights_hbm, held_ref, sem):
    fetch = pltpu.make_async_copy(
        weights_hbm.at[pl.ds(first, held_ref.shape[0])], held_ref, sem
    )
    fetch.start()
    fetch.wait()


def hold(after, weights, first, depth):
    return pl.pallas_call(
        functools.partial(hold_kernel, first),
        in_specs=[THERE, THERE],
        out_specs=WHOLE,
        out_shape=pltpu.VMEM((depth,) + weights.shape[1:], BF16),
        scratch_shapes=[pltpu.SemaphoreType.DMA],
        compiler_params=pltpu.CompilerParams(vmem_limit_bytes=4 * MIB),
        cost_estimate=cost(0, 2 * depth * weights.shape[1] * weights.shape[2]),
        name="hold",
    )(after, pltpu.with_memory_space_constraint(weights, pltpu.HBM))


def gate_up_kernel(
    near_ref, far_ref, a_ref, b_ref, c_ref, weights_hbm, sums_ref, spread, last_ref, sem
):
    held = (a_ref, b_ref, c_ref, last_ref)
    first = sum(part.shape[0] for part in held[:-1])
    fetch = pltpu.make_async_copy(
        weights_hbm.at[pl.ds(first, last_ref.shape[0])], last_ref, sem
    )
    fetch.start()
    depth, _, units = weights_hbm.shape
    rows = near_ref.shape[0] * near_ref.shape[1]
    lanes = 128
    source = lax.broadcasted_iota(jnp.int32, (lanes, 2 * lanes), 0)
    goal = lax.broadcasted_iota(jnp.int32, (lanes, 2 * lanes), 1)
    even = (goal == 2 * source).astype(BF16)
    odd = (goal == 2 * source + 1).astype(BF16)
    x = jnp.concatenate([near_ref[...].reshape(rows, depth), far_ref[...].reshape(rows, depth)])
    rows = 2 * rows
    for b in range(depth // lanes):
        part = x[:, b * lanes : (b + 1) * lanes]
        to = slice(2 * b * lanes, 2 * (b + 1) * lanes)
        spread[:rows, to] = jnp.dot(part, even, preferred_element_type=F32).astype(BF16)
        spread[rows:, to] = jnp.dot(part, odd, preferred_element_type=F32).astype(BF16)
    total = jnp.zeros((2 * rows, units), F32)
    start = 0
    for part in held:
        if part is last_ref:
            fetch.wait()
        end = start + 2 * part.shape[0]
        total += jnp.dot(
            spread[:, start:end],
            part[...].reshape(end - start, units),
            preferred_element_type=F32,
        )
        start = end
    sums_ref[...] = total.astype(BF16)


def gate_up_sums(near, far, held, weights):
    rows = 2 * near.shape[0] * near.shape[1]
    depth, _, units = weights.shape
    rest = depth - sum(part.shape[0] for part in held)
    held = [pltpu.with_memory_space_constraint(part, pltpu.VMEM) for part in held]
    return pl.pallas_call(
        gate_up_kernel,
        in_specs=[WHOLE] * 5 + [THERE],
        out_specs=WHOLE,
        out_shape=jax.ShapeDtypeStruct((2 * rows, units), BF16),
        scratch_shapes=[
            pltpu.VMEM((2 * rows, 2 * depth), BF16),
            pltpu.VMEM((rest,) + weights.shape[1:], BF16),
            pltpu.SemaphoreType.DMA,
        ],
        compiler_params=pltpu.CompilerParams(vmem_limit_bytes=16 * MIB),
        cost_estimate=cost(4 * rows * weights.size, 2 * weights.size),
        name="gate_up_sums",
    )(near, far, *held, pltpu.with_memory_space_constraint(weights, pltpu.HBM))


def hidden_kernel(own_ref, other_ref, out_ref):
    rows = out_ref.shape[0]
    summed = own_ref[...].astype(F32) + other_ref[...].astype(F32)
    gate, up = (summed[:rows], summed[rows:])
    out_ref[...] = (gate / (1.0 + jnp.exp(-gate)) * up).astype(BF16)


def hidden_units(own, other):
    rows, units = own.shape
    return pl.pallas_call(
        hidden_kernel,
        in_specs=[WHOLE] * 2,
        out_specs=WHOLE,
        out_shape=jax.ShapeDtypeStruct((rows // 2, units), BF16),
        compiler_params=pltpu.CompilerParams(vmem_limit_bytes=8 * MIB),
        cost_estimate=cost(4 * own.size, 5 * own.size, own.size // 2),
        name="hidden_units",
    )(own, other)


def down_own_kernel(hidden_ref, down_ref, out_ref):
    units = hidden_ref.shape[1]
    first = pl.multiple_of(lax.axis_index("ctx") * units, units)
    out_ref[...] = jnp.dot(
        hidden_ref[...], down_ref[pl.ds(first, units), :], preferred_element_type=F32
    )


def down_other_kernel(hidden_ref, down_ref, own_ref, out_ref):
    units = hidden_ref.shape[1]
    first = pl.multiple_of((1 - lax.axis_index("ctx")) * units, units)
    experts = lax.axis_size("exp")
    rows = out_ref.shape[1]
    other = jnp.dot(hidden_ref[...], down_ref[pl.ds(first, units), :], preferred_element_type=F32)
    pairs = [other[2 * rows * i : 2 * rows * (i + 1)] for i in (1, 0, 3, 2)]
    total = (own_ref[...] + jnp.concatenate(pairs)).astype(BF16)
    for block in range(out_ref.shape[0]):
        ctx = lax.axis_index("ctx") ^ ((block >> 1) & 1)
        exp = lax.axis_index("exp") ^ (2 * (block & 1) + (block >> 2))
        out_ref[ctx * experts + exp] = total[block * rows : (block + 1) * rows]


def down_sums(hidden, down, own=None, peers=None):
    rows, units = hidden.shape
    columns = down.shape[1]
    down = pltpu.with_memory_space_constraint(down, pltpu.VMEM)
    if own is None:
        kernel, operands = (down_own_kernel, (hidden, down))
        out_shape = jax.ShapeDtypeStruct((rows, columns), F32)
    else:
        kernel, operands = (down_other_kernel, (hidden, down, own))
        out_shape = jax.ShapeDtypeStruct((peers, rows // peers, columns), BF16)
    return pl.pallas_call(
        kernel,
        in_specs=[WHOLE] * len(operands),
        out_specs=WHOLE,
        out_shape=out_shape,
        compiler_params=pltpu.CompilerParams(vmem_limit_bytes=8 * MIB),
        cost_estimate=cost(2 * rows * units * columns, 2 * units * columns),
        name="down_own" if own is None else "down_other",
    )(*operands)


def merge_kernel(ids_ref, weight_ref, back_ref, out_ref, table):
    ctx_count, experts, rows, columns = back_ref.shape
    ids, weight = (ids_ref[...], weight_ref[...])
    for e in range(experts):
        table[e : e + 1, :rows] = jnp.sum(
            jnp.where(ids == e, weight, 0.0), axis=0, keepdims=True
        )
    share = jnp.transpose(table[...])
    for c in range(ctx_count):
        total = jnp.zeros((rows, columns), F32)
        for e in range(experts):
            total += share[:rows, e : e + 1] * back_ref[c, e].astype(F32)
        out_ref[:, c * columns : (c + 1) * columns] = total.astype(BF16)


def merge(route_ids, route_weight, back):
    ctx_count, experts, rows, columns = back.shape
    return pl.pallas_call(
        merge_kernel,
        in_specs=[WHOLE] * 3,
        out_specs=WHOLE,
        out_shape=jax.ShapeDtypeStruct((rows, ctx_count * columns), BF16),
        scratch_shapes=[pltpu.VMEM((8, 128), F32)],
        compiler_params=pltpu.CompilerParams(vmem_limit_bytes=8 * MIB),
        cost_estimate=cost(4 * back.size, 2 * back.size),
        name="merge",
    )(jnp.transpose(route_ids), jnp.transpose(route_weight), back)


def on_device(queries, keys, values, log_decay, moe_input, route_ids, route_weight, gate_up, down):
    ctx_count, expert_list = (lax.axis_size("ctx"), lax.axis_size("exp"))
    if (ctx_count, expert_list, lax.axis_size("tp")) != (2, 4, 2) or gate_up.shape[3] % 128:
        return on_device_any(
            queries, keys, values, log_decay, moe_input, route_ids, route_weight, gate_up, down
        )
    peers = ctx_count * expert_list
    swap = [(0, 1), (1, 0)]
    own_tokens = moe_input[None]
    tokens = join(own_tokens, lax.ppermute(own_tokens, "exp", [(e, e ^ 2) for e in range(4)]))
    weights, w_down = (gate_up.reshape(gate_up.shape[1:]), down.reshape(down.shape[1:]))
    quarter = weights.shape[0] // 4
    intra, local, cum, held = attend(queries, keys, values, log_decay, weights, quarter)
    tokens, local = lax.optimization_barrier((tokens, local))
    held_next = hold(tokens, weights, quarter, quarter)
    arrived, held_next = lax.optimization_barrier((lax.ppermute(tokens, "ctx", swap), held_next))
    tokens = join(tokens, arrived)
    held_last = hold(tokens, weights, 2 * quarter, quarter)
    far_tokens = lax.ppermute(tokens, "exp", [(e, e ^ 1) for e in range(4)])
    state = lax.ppermute(local, "ctx", [(0, 1)])
    sums = gate_up_sums(tokens, far_tokens, (held, held_next, held_last), weights)
    hidden = hidden_units(sums, lax.ppermute(sums, "tp", swap))
    hidden_other = lax.ppermute(hidden, "ctx", swap)
    own = down_sums(hidden, w_down)
    expert_out = down_sums(hidden_other, w_down, own, peers)
    back = lax.all_to_all(expert_out, ("ctx", "exp"), split_axis=0, concat_axis=0, tiled=True)
    attended = finish(queries, intra, cum, state)
    back = back.reshape((ctx_count, expert_list) + back.shape[1:])
    return (attended, merge(route_ids, route_weight, back))


def solution(mesh):
    in_specs = (
        P(("groups", "ctx"), ("exp", "tp")),
        P(("groups", "ctx"), ("exp", "tp")),
        P(("groups", "ctx"), ("exp", "tp")),
        P(("groups", "ctx"), ("exp", "tp")),
        P(("groups", "ctx", "exp"), "tp"),
        P(("groups", "ctx", "exp"), None),
        P(("groups", "ctx", "exp"), None),
        P("exp", "tp", None, "ctx"),
        P("exp", None, ("tp", "ctx")),
    )
    out_specs = (P(("groups", "ctx"), ("exp", "tp")), P(("groups", "ctx", "exp"), "tp"))
    return jax.shard_map(
        on_device, mesh=mesh, in_specs=in_specs, out_specs=out_specs, check_vma=False
    )
```

```python
import functools

import jax
import jax.numpy as jnp
from jax import lax
from jax.experimental import pallas as pl
from jax.experimental.pallas import tpu as pltpu
from jax.sharding import PartitionSpec as P

F32, BF16 = (jnp.float32, jnp.bfloat16)
WHOLE = pl.BlockSpec(memory_space=pltpu.VMEM)
SCALARS = pl.BlockSpec(memory_space=pltpu.SMEM)
THERE = pl.BlockSpec(memory_space=pl.ANY)
MIB = 1 << 20


def prefix(shard, axis, combine, identity):
    devices, here = (lax.axis_size(axis), lax.axis_index(axis))
    everything = jax.tree.map(
        lambda part, kind: lax.all_gather(part.astype(kind), axis),
        shard,
        (jnp.bfloat16, jnp.bfloat16),
    )
    start = jax.tree.map(
        lambda part, zero: jnp.broadcast_to(jnp.asarray(zero, part.dtype), part.shape),
        shard,
        identity,
    )

    def step(k, before):
        reached = k < here
        new = combine(
            before, jax.tree.map(lambda part, own: part[k].astype(own.dtype), everything, shard)
        )
        return jax.tree.map(lambda a, b: jnp.where(reached, a, b), new, before)

    return lax.fori_loop(0, devices, step, start)


def block_terms(queries, keys, values, log_decay):
    rows = queries.shape[0]
    heads = log_decay.shape[1]
    qb = queries.reshape(rows, heads, -1)
    kb = keys.reshape(rows, heads, -1)
    vb = values.reshape(rows, heads, -1)
    cum = jnp.cumsum(log_decay, axis=0)
    diff = jnp.transpose(cum)[:, :, None] - jnp.transpose(cum)[:, None, :]
    causal = jnp.arange(rows)[:, None] >= jnp.arange(rows)[None, :]
    decay = jnp.where(causal[None, :, :], jnp.exp(jnp.minimum(diff, 0.0)), 0.0)
    scores = jnp.einsum("thd,shd->hts", qb, kb, preferred_element_type=jnp.float32)
    weights = (scores * decay).astype(jnp.bfloat16)
    intra = jnp.einsum("hts,shd->thd", weights, vb, preferred_element_type=jnp.float32)
    last = cum[-1]
    kscaled = kb.astype(jnp.float32) * jnp.exp(last[None, :] - cum)[:, :, None]
    local = jnp.einsum(
        "shd,she->hde", kscaled, vb.astype(jnp.float32), precision=lax.Precision.HIGHEST
    )
    return (qb, cum, intra, local, jnp.exp(last))


def chain_states(preceding_positions, later):
    return (
        preceding_positions[0] * later[0],
        later[0][:, None, None] * preceding_positions[1] + later[1],
    )


def route_slots(route_ids, expert_list, slots_each):
    flat_ids = route_ids.reshape(-1)
    onehot = (flat_ids[:, None] == jnp.arange(expert_list)[None, :]).astype(jnp.int32)
    slot = jnp.sum((jnp.cumsum(onehot, axis=0) - 1) * onehot, axis=1)
    target = flat_ids * slots_each + slot
    pick = jnp.arange(expert_list * slots_each)[:, None] == target[None, :]
    return (target, pick)


def on_device_any(queries, keys, values, log_decay, moe_input, route_ids, route_weight, gate_up, down):
    qb, cum, intra, local, totals = block_terms(queries, keys, values, log_decay)
    heads = log_decay.shape[1]
    width = local.shape[1]
    identity = (jnp.ones((heads,), jnp.float32), jnp.zeros((heads, width, width), jnp.float32))
    entering = prefix((totals, local), "ctx", chain_states, identity)
    qscaled = qb.astype(jnp.float32) * jnp.exp(cum)[:, :, None]
    inter = jnp.einsum("thd,hde->the", qscaled, entering[1], precision=lax.Precision.HIGHEST)
    mixed = intra + inter
    normed = mixed * lax.rsqrt(jnp.mean(mixed * mixed, axis=-1, keepdims=True) + 1e-06)
    attended = normed.astype(jnp.bfloat16).reshape(queries.shape)
    expert_list = lax.axis_size("exp")
    ctx_count = lax.axis_size("ctx")
    tok_rows = moe_input.shape[0]
    half_width = moe_input.shape[1]
    slots_each = min(tok_rows, tok_rows * 2 // expert_list + tok_rows // 4)
    target, pick = route_slots(route_ids, expert_list, slots_each)
    doubled = jnp.repeat(moe_input, 2, axis=0)
    send = jnp.dot(pick.astype(jnp.bfloat16), doubled, preferred_element_type=jnp.float32)
    send = send.astype(jnp.bfloat16).reshape(expert_list, slots_each, half_width)
    arrived = lax.all_to_all(send, "exp", split_axis=0, concat_axis=0, tiled=True)
    slot_rows = arrived.reshape(expert_list * slots_each, half_width)
    w_both = gate_up.reshape(half_width, -1)
    ff_local = w_both.shape[1] // 2
    partial_value = jnp.dot(
        lax.all_gather(slot_rows, "ctx", axis=0, tiled=True),
        w_both,
        preferred_element_type=jnp.float32,
    )
    summed = lax.psum(partial_value.astype(jnp.bfloat16), "tp").astype(jnp.float32)
    hidden = (jax.nn.silu(summed[:, :ff_local]) * summed[:, ff_local:]).astype(jnp.bfloat16)
    w_down = down.reshape(down.shape[1], down.shape[2])
    expert_out = jnp.dot(
        lax.all_gather(hidden, "ctx", axis=1, tiled=True),
        w_down,
        preferred_element_type=jnp.float32,
    ).astype(jnp.bfloat16)
    col_width = expert_out.shape[1]
    stacked = expert_out.reshape(ctx_count, expert_list, slots_each, col_width)
    back = lax.all_to_all(
        lax.all_to_all(stacked, "ctx", split_axis=0, concat_axis=3, tiled=True),
        "exp",
        split_axis=1,
        concat_axis=1,
        tiled=True,
    )
    flat = back.reshape(expert_list * slots_each, half_width)
    selected_routes = flat[target].astype(jnp.float32).reshape(tok_rows, 2, half_width)
    merged_output = jnp.sum(selected_routes * route_weight[:, :, None], axis=1)
    return (attended, merged_output.astype(jnp.bfloat16))

def cost(flops, read, transcendentals=0):
    return pl.CostEstimate(flops=flops, bytes_accessed=read, transcendentals=transcendentals)


def head_columns(h, width):
    return slice(h * width, (h + 1) * width)


def attend_kernel(
    heads, q_hbm, k_hbm, v_hbm, decay_hbm, weights_hbm, intra_ref, local_ref, cum_ref, held_ref,
    q_ref, k_ref, v_ref, decay_ref, sems,
):
    pairs = (
        (decay_hbm, decay_ref),
        (q_hbm, q_ref),
        (k_hbm, k_ref),
        (v_hbm, v_ref),
        (weights_hbm.at[pl.ds(0, held_ref.shape[0])], held_ref),
    )
    fetches = [pltpu.make_async_copy(a, b, sems.at[i]) for i, (a, b) in enumerate(pairs)]
    for fetch in fetches:
        fetch.start()
    rows = q_ref.shape[0]
    width = q_ref.shape[1] // heads
    s_at = lax.broadcasted_iota(jnp.int32, (rows, rows), 0)
    t_at = lax.broadcasted_iota(jnp.int32, (rows, rows), 1)
    before = (s_at <= t_at).astype(F32)
    fetches[0].wait()
    cum_t = jnp.dot(
        decay_ref[...], before, precision=lax.Precision.HIGHEST, preferred_element_type=F32
    )
    cum = jnp.transpose(cum_t)
    cum_ref[...] = cum
    for fetch in fetches[1:4]:
        fetch.wait()
    for h in range(heads):
        at = head_columns(h, width)
        q, k, v = (q_ref[:, at], k_ref[:, at], v_ref[:, at])
        column, row = (cum[:, h : h + 1], cum_t[h : h + 1, :])
        decay = jnp.where(s_at >= t_at, jnp.exp(jnp.minimum(column - row, 0.0)), 0.0)
        scores = lax.dot_general(q, k, (((1,), (1,)), ((), ())), preferred_element_type=F32)
        intra_ref[:, at] = jnp.dot(
            (scores * decay).astype(BF16), v, preferred_element_type=F32
        )
        rest = jnp.exp(cum[rows - 1 :, h : h + 1] - column)
        scaled = (k.astype(F32) * rest).astype(BF16)
        local = lax.dot_general(scaled, v, (((0,), (0,)), ((), ())), preferred_element_type=F32)
        local_ref[h * width : (h + 1) * width, :] = local.astype(BF16)
    fetches[4].wait()


def attend(queries, keys, values, log_decay, weights, depth):
    rows, heads = log_decay.shape
    width = queries.shape[1] // heads
    operands = (queries, keys, values, jnp.transpose(log_decay), weights)
    return pl.pallas_call(
        functools.partial(attend_kernel, heads),
        in_specs=[THERE] * 5,
        out_specs=[WHOLE] * 4,
        out_shape=[
            jax.ShapeDtypeStruct(queries.shape, F32),
            jax.ShapeDtypeStruct((heads * width, width), BF16),
            jax.ShapeDtypeStruct((rows, heads), F32),
            pltpu.VMEM((depth,) + weights.shape[1:], BF16),
        ],
        scratch_shapes=[pltpu.VMEM(queries.shape, BF16)] * 3
        + [pltpu.VMEM((heads, rows), F32), pltpu.SemaphoreType.DMA((5,))],
        compiler_params=pltpu.CompilerParams(vmem_limit_bytes=8 * MIB),
        cost_estimate=cost(10**10, 6 * queries.size, heads * rows * rows),
        name="attend",
    )(*(pltpu.with_memory_space_constraint(x, pltpu.HBM) for x in operands))


def finish_kernel(heads, q_ref, intra_ref, cum_ref, state_ref, out_ref):
    width = q_ref.shape[1] // heads
    entered = lax.axis_index("ctx") > 0
    for h in range(heads):
        at = head_columns(h, width)
        grown = jnp.where(entered, jnp.exp(cum_ref[:, h : h + 1]), 0.0)
        state = state_ref[h * width : (h + 1) * width, :]
        mixed = intra_ref[:, at] + grown * jnp.dot(
            q_ref[:, at], state, preferred_element_type=F32
        )
        mean = jnp.mean(mixed * mixed, axis=1, keepdims=True)
        out_ref[:, at] = (mixed * lax.rsqrt(mean + 1e-06)).astype(BF16)


def finish(queries, intra, cum, state):
    rows, heads = cum.shape
    return pl.pallas_call(
        functools.partial(finish_kernel, heads),
        in_specs=[WHOLE] * 4,
        out_specs=WHOLE,
        out_shape=jax.ShapeDtypeStruct(queries.shape, BF16),
        compiler_params=pltpu.CompilerParams(vmem_limit_bytes=8 * MIB),
        cost_estimate=cost(2 * queries.size * 128, 10 * queries.size, queries.size),
        name="finish",
    )(queries, intra, cum, state)


def join_kernel(first_ref, second_ref, out_ref):
    count = first_ref.shape[0]
    out_ref[:count] = first_ref[...]
    out_ref[count:] = second_ref[...]


def join(first, second):
    return pl.pallas_call(
        join_kernel,
        in_specs=[WHOLE] * 2,
        out_specs=WHOLE,
        out_shape=jax.ShapeDtypeStruct((2 * first.shape[0],) + first.shape[1:], first.dtype),
        compiler_params=pltpu.CompilerParams(vmem_limit_bytes=4 * MIB),
        cost_estimate=cost(3 * 10**9, 8 * first.size),
        name="join",
    )(first, second)


def hold_kernel(first, after_ref, weights_hbm, held_ref, sem):
    fetch = pltpu.make_async_copy(
        weights_hbm.at[pl.ds(first, held_ref.shape[0])], held_ref, sem
    )
    fetch.start()
    fetch.wait()


def hold(after, weights, first, depth):
    return pl.pallas_call(
        functools.partial(hold_kernel, first),
        in_specs=[THERE, THERE],
        out_specs=WHOLE,
        out_shape=pltpu.VMEM((depth,) + weights.shape[1:], BF16),
        scratch_shapes=[pltpu.SemaphoreType.DMA],
        compiler_params=pltpu.CompilerParams(vmem_limit_bytes=4 * MIB),
        cost_estimate=cost(0, 2 * depth * weights.shape[1] * weights.shape[2]),
        name="hold",
    )(after, pltpu.with_memory_space_constraint(weights, pltpu.HBM))


def gate_up_kernel(
    near_ref, far_ref, a_ref, b_ref, c_ref, weights_hbm, sums_ref, spread, last_ref, sem
):
    held = (a_ref, b_ref, c_ref, last_ref)
    first = sum(part.shape[0] for part in held[:-1])
    fetch = pltpu.make_async_copy(
        weights_hbm.at[pl.ds(first, last_ref.shape[0])], last_ref, sem
    )
    fetch.start()
    depth, _, units = weights_hbm.shape
    rows = near_ref.shape[0] * near_ref.shape[1]
    lanes = 128
    source = lax.broadcasted_iota(jnp.int32, (lanes, 4 * lanes), 0)
    goal = lax.broadcasted_iota(jnp.int32, (lanes, 4 * lanes), 1)
    places = jnp.where(goal < 2 * lanes, 2 * source, 2 * source + 2 * lanes + 1)
    x = jnp.concatenate([near_ref[...].reshape(rows, depth), far_ref[...].reshape(rows, depth)])
    rows = 2 * rows
    blocks = depth // lanes
    stacked = jnp.concatenate([x[:, b * lanes : (b + 1) * lanes] for b in range(blocks)])
    wide = jnp.dot(stacked, (goal == places).astype(BF16), preferred_element_type=F32)
    wide = wide.astype(BF16)
    for b in range(blocks):
        to = slice(2 * b * lanes, 2 * (b + 1) * lanes)
        spread[:rows, to] = wide[b * rows : (b + 1) * rows, : 2 * lanes]
        spread[rows:, to] = wide[b * rows : (b + 1) * rows, 2 * lanes :]
    total = jnp.zeros((2 * rows, units), F32)
    start = 0
    for part in held:
        if part is last_ref:
            fetch.wait()
        end = start + 2 * part.shape[0]
        total += jnp.dot(
            spread[:, start:end],
            part[...].reshape(end - start, units),
            preferred_element_type=F32,
        )
        start = end
    sums_ref[...] = total.astype(BF16)


def gate_up_sums(near, far, held, weights):
    rows = 2 * near.shape[0] * near.shape[1]
    depth, _, units = weights.shape
    rest = depth - sum(part.shape[0] for part in held)
    held = [pltpu.with_memory_space_constraint(part, pltpu.VMEM) for part in held]
    return pl.pallas_call(
        gate_up_kernel,
        in_specs=[WHOLE] * 5 + [THERE],
        out_specs=WHOLE,
        out_shape=jax.ShapeDtypeStruct((2 * rows, units), BF16),
        scratch_shapes=[
            pltpu.VMEM((2 * rows, 2 * depth), BF16),
            pltpu.VMEM((rest,) + weights.shape[1:], BF16),
            pltpu.SemaphoreType.DMA,
        ],
        compiler_params=pltpu.CompilerParams(vmem_limit_bytes=16 * MIB),
        cost_estimate=cost(4 * rows * weights.size, 2 * weights.size),
        name="gate_up_sums",
    )(near, far, *held, pltpu.with_memory_space_constraint(weights, pltpu.HBM))


def hidden_kernel(own_ref, other_ref, out_ref, part_ref):
    rows = out_ref.shape[0]
    summed = own_ref[...].astype(F32) + other_ref[...].astype(F32)
    gate, up = (summed[:rows], summed[rows:])
    hidden = (gate / (1.0 + jnp.exp(-gate)) * up).astype(BF16)
    out_ref[...] = hidden
    half = part_ref.shape[1]
    part_ref[...] = jnp.where(lax.axis_index("tp") == 0, hidden[:, :half], hidden[:, half:])


def hidden_units(own, other):
    rows, units = own.shape
    return pl.pallas_call(
        hidden_kernel,
        in_specs=[WHOLE] * 2,
        out_specs=[WHOLE] * 2,
        out_shape=[
            jax.ShapeDtypeStruct((rows // 2, units), BF16),
            jax.ShapeDtypeStruct((rows // 2, units // 2), BF16),
        ],
        compiler_params=pltpu.CompilerParams(vmem_limit_bytes=8 * MIB),
        cost_estimate=cost(4 * own.size, 5 * own.size, own.size // 2),
        name="hidden_units",
    )(own, other)


def down_own_kernel(hidden_ref, down_ref, out_ref):
    units = hidden_ref.shape[1]
    first = pl.multiple_of(lax.axis_index("ctx") * units, units)
    out_ref[...] = jnp.dot(
        hidden_ref[...], down_ref[pl.ds(first, units), :], preferred_element_type=F32
    )


def other_product(part, down_ref, core):
    units = part.shape[1]
    first = pl.multiple_of((2 * (1 - lax.axis_index("ctx")) + core) * units, units)
    return jnp.dot(part, down_ref[pl.ds(first, units), :], preferred_element_type=F32)


def down_near_kernel(part_ref, down_ref, own_ref, out_ref):
    other = other_product(part_ref[...], down_ref, lax.axis_index("tp"))
    count = other.shape[0] // 4
    pairs = [other[count * i : count * (i + 1)] for i in (1, 0, 3, 2)]
    out_ref[...] = own_ref[...] + jnp.concatenate(pairs)


def down_far_kernel(part_ref, down_ref, own_ref, out_ref):
    experts = lax.axis_size("exp")
    rows = out_ref.shape[1]
    other = other_product(part_ref[...], down_ref, 1 - lax.axis_index("tp"))
    pairs = [other[2 * rows * i : 2 * rows * (i + 1)] for i in (1, 0, 3, 2)]
    total = (own_ref[...] + jnp.concatenate(pairs)).astype(BF16)
    for block in range(out_ref.shape[0]):
        ctx = lax.axis_index("ctx") ^ ((block >> 1) & 1)
        exp = lax.axis_index("exp") ^ (2 * (block & 1) + (block >> 2))
        out_ref[ctx * experts + exp] = total[block * rows : (block + 1) * rows]


def down_sums(kernel, shape, dtype, hidden, down, *sums):
    rows, units = hidden.shape
    columns = down.shape[1]
    down = pltpu.with_memory_space_constraint(down, pltpu.VMEM)
    return pl.pallas_call(
        kernel,
        in_specs=[WHOLE] * (2 + len(sums)),
        out_specs=WHOLE,
        out_shape=jax.ShapeDtypeStruct(shape, dtype),
        compiler_params=pltpu.CompilerParams(vmem_limit_bytes=8 * MIB),
        cost_estimate=cost(2 * rows * units * columns, 2 * units * columns),
        name=kernel.__name__[:-7],
    )(hidden, down, *sums)


def merge_kernel(ids_ref, weight_ref, back_ref, out_ref, table):
    ctx_count, experts, rows, columns = back_ref.shape
    ids, weight = (ids_ref[...], weight_ref[...])
    for e in range(experts):
        table[e : e + 1, :rows] = jnp.sum(
            jnp.where(ids == e, weight, 0.0), axis=0, keepdims=True
        )
    share = jnp.transpose(table[...])
    for c in range(ctx_count):
        total = jnp.zeros((rows, columns), F32)
        for e in range(experts):
            total += share[:rows, e : e + 1] * back_ref[c, e].astype(F32)
        out_ref[:, c * columns : (c + 1) * columns] = total.astype(BF16)


def merge(route_ids, route_weight, back):
    ctx_count, experts, rows, columns = back.shape
    return pl.pallas_call(
        merge_kernel,
        in_specs=[WHOLE] * 3,
        out_specs=WHOLE,
        out_shape=jax.ShapeDtypeStruct((rows, ctx_count * columns), BF16),
        scratch_shapes=[pltpu.VMEM((8, 128), F32)],
        compiler_params=pltpu.CompilerParams(vmem_limit_bytes=8 * MIB),
        cost_estimate=cost(4 * back.size, 2 * back.size),
        name="merge",
    )(jnp.transpose(route_ids), jnp.transpose(route_weight), back)


def on_device(queries, keys, values, log_decay, moe_input, route_ids, route_weight, gate_up, down):
    ctx_count, expert_list = (lax.axis_size("ctx"), lax.axis_size("exp"))
    if (ctx_count, expert_list, lax.axis_size("tp")) != (2, 4, 2) or gate_up.shape[3] % 128:
        return on_device_any(
            queries, keys, values, log_decay, moe_input, route_ids, route_weight, gate_up, down
        )
    peers = ctx_count * expert_list
    swap = [(0, 1), (1, 0)]
    own_tokens = moe_input[None]
    tokens = join(own_tokens, lax.ppermute(own_tokens, "exp", [(e, e ^ 2) for e in range(4)]))
    weights, w_down = (gate_up.reshape(gate_up.shape[1:]), down.reshape(down.shape[1:]))
    quarter = weights.shape[0] // 4
    intra, local, cum, held = attend(queries, keys, values, log_decay, weights, quarter)
    tokens, local = lax.optimization_barrier((tokens, local))
    held_next = hold(tokens, weights, quarter, quarter)
    arrived, held_next = lax.optimization_barrier((lax.ppermute(tokens, "ctx", swap), held_next))
    tokens = join(tokens, arrived)
    held_last = hold(tokens, weights, 2 * quarter, quarter)
    far_tokens = lax.ppermute(tokens, "exp", [(e, e ^ 1) for e in range(4)])
    sums = gate_up_sums(tokens, far_tokens, (held, held_next, held_last), weights)
    hidden, part = hidden_units(sums, lax.ppermute(sums, "tp", swap))
    part = lax.ppermute(part, "ctx", swap)
    sums_shape = (hidden.shape[0], w_down.shape[1])
    total = down_sums(down_own_kernel, sums_shape, F32, hidden, w_down)
    total, local = lax.optimization_barrier((total, local))
    state = lax.ppermute(local, "ctx", swap)
    part_far = lax.ppermute(part, "tp", swap)
    total = down_sums(down_near_kernel, sums_shape, F32, part, w_down, total)
    rows = moe_input.shape[0]
    expert_out = down_sums(
        down_far_kernel, (peers, rows, sums_shape[1]), BF16, part_far, w_down, total
    )
    back = lax.all_to_all(expert_out, ("ctx", "exp"), split_axis=0, concat_axis=0, tiled=True)
    attended = finish(queries, intra, cum, state)
    back = back.reshape((ctx_count, expert_list) + back.shape[1:])
    return (attended, merge(route_ids, route_weight, back))


def solution(mesh):
    in_specs = (
        P(("groups", "ctx"), ("exp", "tp")),
        P(("groups", "ctx"), ("exp", "tp")),
        P(("groups", "ctx"), ("exp", "tp")),
        P(("groups", "ctx"), ("exp", "tp")),
        P(("groups", "ctx", "exp"), "tp"),
        P(("groups", "ctx", "exp"), None),
        P(("groups", "ctx", "exp"), None),
        P("exp", "tp", None, "ctx"),
        P("exp", None, ("tp", "ctx")),
    )
    out_specs = (P(("groups", "ctx"), ("exp", "tp")), P(("groups", "ctx", "exp"), "tp"))
    return jax.shard_map(
        on_device, mesh=mesh, in_specs=in_specs, out_specs=out_specs, check_vma=False
    )
```

```python
import functools

import jax
import jax.numpy as jnp
from jax import lax
from jax.experimental import pallas as pl
from jax.experimental.pallas import tpu as pltpu
from jax.sharding import PartitionSpec as P

F32, BF16 = (jnp.float32, jnp.bfloat16)
WHOLE = pl.BlockSpec(memory_space=pltpu.VMEM)
SCALARS = pl.BlockSpec(memory_space=pltpu.SMEM)
THERE = pl.BlockSpec(memory_space=pl.ANY)
MIB = 1 << 20


def prefix(shard, axis, combine, identity):
    devices, here = (lax.axis_size(axis), lax.axis_index(axis))
    everything = jax.tree.map(
        lambda part, kind: lax.all_gather(part.astype(kind), axis),
        shard,
        (jnp.bfloat16, jnp.bfloat16),
    )
    start = jax.tree.map(
        lambda part, zero: jnp.broadcast_to(jnp.asarray(zero, part.dtype), part.shape),
        shard,
        identity,
    )

    def step(k, before):
        reached = k < here
        new = combine(
            before, jax.tree.map(lambda part, own: part[k].astype(own.dtype), everything, shard)
        )
        return jax.tree.map(lambda a, b: jnp.where(reached, a, b), new, before)

    return lax.fori_loop(0, devices, step, start)


def block_terms(queries, keys, values, log_decay):
    rows = queries.shape[0]
    heads = log_decay.shape[1]
    qb = queries.reshape(rows, heads, -1)
    kb = keys.reshape(rows, heads, -1)
    vb = values.reshape(rows, heads, -1)
    cum = jnp.cumsum(log_decay, axis=0)
    diff = jnp.transpose(cum)[:, :, None] - jnp.transpose(cum)[:, None, :]
    causal = jnp.arange(rows)[:, None] >= jnp.arange(rows)[None, :]
    decay = jnp.where(causal[None, :, :], jnp.exp(jnp.minimum(diff, 0.0)), 0.0)
    scores = jnp.einsum("thd,shd->hts", qb, kb, preferred_element_type=jnp.float32)
    weights = (scores * decay).astype(jnp.bfloat16)
    intra = jnp.einsum("hts,shd->thd", weights, vb, preferred_element_type=jnp.float32)
    last = cum[-1]
    kscaled = kb.astype(jnp.float32) * jnp.exp(last[None, :] - cum)[:, :, None]
    local = jnp.einsum(
        "shd,she->hde", kscaled, vb.astype(jnp.float32), precision=lax.Precision.HIGHEST
    )
    return (qb, cum, intra, local, jnp.exp(last))


def chain_states(preceding_positions, later):
    return (
        preceding_positions[0] * later[0],
        later[0][:, None, None] * preceding_positions[1] + later[1],
    )


def route_slots(route_ids, expert_list, slots_each):
    flat_ids = route_ids.reshape(-1)
    onehot = (flat_ids[:, None] == jnp.arange(expert_list)[None, :]).astype(jnp.int32)
    slot = jnp.sum((jnp.cumsum(onehot, axis=0) - 1) * onehot, axis=1)
    target = flat_ids * slots_each + slot
    pick = jnp.arange(expert_list * slots_each)[:, None] == target[None, :]
    return (target, pick)


def on_device_any(queries, keys, values, log_decay, moe_input, route_ids, route_weight, gate_up, down):
    qb, cum, intra, local, totals = block_terms(queries, keys, values, log_decay)
    heads = log_decay.shape[1]
    width = local.shape[1]
    identity = (jnp.ones((heads,), jnp.float32), jnp.zeros((heads, width, width), jnp.float32))
    entering = prefix((totals, local), "ctx", chain_states, identity)
    qscaled = qb.astype(jnp.float32) * jnp.exp(cum)[:, :, None]
    inter = jnp.einsum("thd,hde->the", qscaled, entering[1], precision=lax.Precision.HIGHEST)
    mixed = intra + inter
    normed = mixed * lax.rsqrt(jnp.mean(mixed * mixed, axis=-1, keepdims=True) + 1e-06)
    attended = normed.astype(jnp.bfloat16).reshape(queries.shape)
    expert_list = lax.axis_size("exp")
    ctx_count = lax.axis_size("ctx")
    tok_rows = moe_input.shape[0]
    half_width = moe_input.shape[1]
    slots_each = min(tok_rows, tok_rows * 2 // expert_list + tok_rows // 4)
    target, pick = route_slots(route_ids, expert_list, slots_each)
    doubled = jnp.repeat(moe_input, 2, axis=0)
    send = jnp.dot(pick.astype(jnp.bfloat16), doubled, preferred_element_type=jnp.float32)
    send = send.astype(jnp.bfloat16).reshape(expert_list, slots_each, half_width)
    arrived = lax.all_to_all(send, "exp", split_axis=0, concat_axis=0, tiled=True)
    slot_rows = arrived.reshape(expert_list * slots_each, half_width)
    w_both = gate_up.reshape(half_width, -1)
    ff_local = w_both.shape[1] // 2
    partial_value = jnp.dot(
        lax.all_gather(slot_rows, "ctx", axis=0, tiled=True),
        w_both,
        preferred_element_type=jnp.float32,
    )
    summed = lax.psum(partial_value.astype(jnp.bfloat16), "tp").astype(jnp.float32)
    hidden = (jax.nn.silu(summed[:, :ff_local]) * summed[:, ff_local:]).astype(jnp.bfloat16)
    w_down = down.reshape(down.shape[1], down.shape[2])
    expert_out = jnp.dot(
        lax.all_gather(hidden, "ctx", axis=1, tiled=True),
        w_down,
        preferred_element_type=jnp.float32,
    ).astype(jnp.bfloat16)
    col_width = expert_out.shape[1]
    stacked = expert_out.reshape(ctx_count, expert_list, slots_each, col_width)
    back = lax.all_to_all(
        lax.all_to_all(stacked, "ctx", split_axis=0, concat_axis=3, tiled=True),
        "exp",
        split_axis=1,
        concat_axis=1,
        tiled=True,
    )
    flat = back.reshape(expert_list * slots_each, half_width)
    selected_routes = flat[target].astype(jnp.float32).reshape(tok_rows, 2, half_width)
    merged_output = jnp.sum(selected_routes * route_weight[:, :, None], axis=1)
    return (attended, merged_output.astype(jnp.bfloat16))

def cost(flops, read, transcendentals=0):
    return pl.CostEstimate(flops=flops, bytes_accessed=read, transcendentals=transcendentals)


def head_columns(h, width):
    return slice(h * width, (h + 1) * width)


def attend_kernel(
    heads, q_hbm, k_hbm, v_hbm, decay_hbm, weights_hbm, intra_ref, local_ref, cum_ref, held_ref,
    q_ref, k_ref, v_ref, decay_ref, sems,
):
    pairs = (
        (decay_hbm, decay_ref),
        (q_hbm, q_ref),
        (k_hbm, k_ref),
        (v_hbm, v_ref),
        (weights_hbm.at[pl.ds(0, held_ref.shape[0])], held_ref),
    )
    fetches = [pltpu.make_async_copy(a, b, sems.at[i]) for i, (a, b) in enumerate(pairs)]
    for fetch in fetches:
        fetch.start()
    rows = q_ref.shape[0]
    width = q_ref.shape[1] // heads
    s_at = lax.broadcasted_iota(jnp.int32, (rows, rows), 0)
    t_at = lax.broadcasted_iota(jnp.int32, (rows, rows), 1)
    before = (s_at <= t_at).astype(F32)
    fetches[0].wait()
    cum_t = jnp.dot(
        decay_ref[...], before, precision=lax.Precision.HIGHEST, preferred_element_type=F32
    )
    cum = jnp.transpose(cum_t)
    cum_ref[...] = cum
    for fetch in fetches[1:4]:
        fetch.wait()
    for h in range(heads):
        at = head_columns(h, width)
        q, k, v = (q_ref[:, at], k_ref[:, at], v_ref[:, at])
        column, row = (cum[:, h : h + 1], cum_t[h : h + 1, :])
        decay = jnp.where(s_at >= t_at, jnp.exp(jnp.minimum(column - row, 0.0)), 0.0)
        scores = lax.dot_general(q, k, (((1,), (1,)), ((), ())), preferred_element_type=F32)
        intra_ref[:, at] = jnp.dot(
            (scores * decay).astype(BF16), v, preferred_element_type=F32
        )
        rest = jnp.exp(cum[rows - 1 :, h : h + 1] - column)
        scaled = (k.astype(F32) * rest).astype(BF16)
        local = lax.dot_general(scaled, v, (((0,), (0,)), ((), ())), preferred_element_type=F32)
        local_ref[h * width : (h + 1) * width, :] = local.astype(BF16)
    fetches[4].wait()


def attend(queries, keys, values, log_decay, weights, depth):
    rows, heads = log_decay.shape
    width = queries.shape[1] // heads
    operands = (queries, keys, values, jnp.transpose(log_decay), weights)
    return pl.pallas_call(
        functools.partial(attend_kernel, heads),
        in_specs=[THERE] * 5,
        out_specs=[WHOLE] * 4,
        out_shape=[
            jax.ShapeDtypeStruct(queries.shape, F32),
            jax.ShapeDtypeStruct((heads * width, width), BF16),
            jax.ShapeDtypeStruct((rows, heads), F32),
            pltpu.VMEM((depth,) + weights.shape[1:], BF16),
        ],
        scratch_shapes=[pltpu.VMEM(queries.shape, BF16)] * 3
        + [pltpu.VMEM((heads, rows), F32), pltpu.SemaphoreType.DMA((5,))],
        compiler_params=pltpu.CompilerParams(vmem_limit_bytes=8 * MIB),
        cost_estimate=cost(10**10, 6 * queries.size, heads * rows * rows),
        name="attend",
    )(*(pltpu.with_memory_space_constraint(x, pltpu.HBM) for x in operands))


def finish_kernel(heads, q_ref, intra_ref, cum_ref, state_ref, out_ref):
    width = q_ref.shape[1] // heads
    entered = lax.axis_index("ctx") > 0
    for h in range(heads):
        at = head_columns(h, width)
        grown = jnp.where(entered, jnp.exp(cum_ref[:, h : h + 1]), 0.0)
        state = state_ref[h * width : (h + 1) * width, :]
        mixed = intra_ref[:, at] + grown * jnp.dot(
            q_ref[:, at], state, preferred_element_type=F32
        )
        mean = jnp.mean(mixed * mixed, axis=1, keepdims=True)
        out_ref[:, at] = (mixed * lax.rsqrt(mean + 1e-06)).astype(BF16)


def finish(queries, intra, cum, state):
    rows, heads = cum.shape
    return pl.pallas_call(
        functools.partial(finish_kernel, heads),
        in_specs=[WHOLE] * 4,
        out_specs=WHOLE,
        out_shape=jax.ShapeDtypeStruct(queries.shape, BF16),
        compiler_params=pltpu.CompilerParams(vmem_limit_bytes=8 * MIB),
        cost_estimate=cost(2 * queries.size * 128, 10 * queries.size, queries.size),
        name="finish",
    )(queries, intra, cum, state)


def join_kernel(*refs):
    out_ref = refs[-1]
    for i, part_ref in enumerate(refs[:-1]):
        out_ref[i : i + 1] = part_ref[...]


def join(*parts):
    return pl.pallas_call(
        join_kernel,
        in_specs=[WHOLE] * len(parts),
        out_specs=WHOLE,
        out_shape=jax.ShapeDtypeStruct((len(parts),) + parts[0].shape[1:], parts[0].dtype),
        compiler_params=pltpu.CompilerParams(vmem_limit_bytes=4 * MIB),
        cost_estimate=cost(0, 16 * parts[0].size),
        name="join",
    )(*parts)


def hold_kernel(first, after_ref, weights_hbm, held_ref, sem):
    fetch = pltpu.make_async_copy(
        weights_hbm.at[pl.ds(first, held_ref.shape[0])], held_ref, sem
    )
    fetch.start()
    fetch.wait()


def hold(after, weights, first, depth):
    return pl.pallas_call(
        functools.partial(hold_kernel, first),
        in_specs=[THERE, THERE],
        out_specs=WHOLE,
        out_shape=pltpu.VMEM((depth,) + weights.shape[1:], BF16),
        scratch_shapes=[pltpu.SemaphoreType.DMA],
        compiler_params=pltpu.CompilerParams(vmem_limit_bytes=4 * MIB),
        cost_estimate=cost(0, 2 * depth * weights.shape[1] * weights.shape[2]),
        name="hold",
    )(after, pltpu.with_memory_space_constraint(weights, pltpu.HBM))


def gate_up_kernel(
    near_ref, far_ref, a_ref, b_ref, weights_hbm, sums_ref, spread, last_ref, sem
):
    held = (a_ref, b_ref, last_ref)
    first = sum(part.shape[0] for part in held[:-1])
    fetch = pltpu.make_async_copy(
        weights_hbm.at[pl.ds(first, last_ref.shape[0])], last_ref, sem
    )
    fetch.start()
    depth, _, units = weights_hbm.shape
    rows = near_ref.shape[0] * near_ref.shape[1]
    lanes = 128
    source = lax.broadcasted_iota(jnp.int32, (lanes, 4 * lanes), 0)
    goal = lax.broadcasted_iota(jnp.int32, (lanes, 4 * lanes), 1)
    places = jnp.where(goal < 2 * lanes, 2 * source, 2 * source + 2 * lanes + 1)
    x = jnp.concatenate([near_ref[...].reshape(rows, depth), far_ref[...].reshape(rows, depth)])
    rows = 2 * rows
    blocks = depth // lanes
    stacked = jnp.concatenate([x[:, b * lanes : (b + 1) * lanes] for b in range(blocks)])
    wide = jnp.dot(stacked, (goal == places).astype(BF16), preferred_element_type=F32)
    wide = wide.astype(BF16)
    for b in range(blocks):
        to = slice(2 * b * lanes, 2 * (b + 1) * lanes)
        spread[:rows, to] = wide[b * rows : (b + 1) * rows, : 2 * lanes]
        spread[rows:, to] = wide[b * rows : (b + 1) * rows, 2 * lanes :]
    total = jnp.zeros((2 * rows, units), F32)
    start = 0
    for part in held:
        if part is last_ref:
            fetch.wait()
        end = start + 2 * part.shape[0]
        total += jnp.dot(
            spread[:, start:end],
            part[...].reshape(end - start, units),
            preferred_element_type=F32,
        )
        start = end
    sums_ref[...] = total.astype(BF16)


def gate_up_sums(near, far, held, weights):
    rows = 2 * near.shape[0] * near.shape[1]
    depth, _, units = weights.shape
    rest = depth - sum(part.shape[0] for part in held)
    held = [pltpu.with_memory_space_constraint(part, pltpu.VMEM) for part in held]
    return pl.pallas_call(
        gate_up_kernel,
        in_specs=[WHOLE] * 4 + [THERE],
        out_specs=WHOLE,
        out_shape=jax.ShapeDtypeStruct((2 * rows, units), BF16),
        scratch_shapes=[
            pltpu.VMEM((2 * rows, 2 * depth), BF16),
            pltpu.VMEM((rest,) + weights.shape[1:], BF16),
            pltpu.SemaphoreType.DMA,
        ],
        compiler_params=pltpu.CompilerParams(vmem_limit_bytes=20 * MIB),
        cost_estimate=cost(4 * rows * weights.size, 2 * weights.size),
        name="gate_up_sums",
    )(near, far, *held, pltpu.with_memory_space_constraint(weights, pltpu.HBM))


def hidden_kernel(own_ref, other_ref, out_ref, part_ref):
    rows = out_ref.shape[0]
    summed = own_ref[...].astype(F32) + other_ref[...].astype(F32)
    gate, up = (summed[:rows], summed[rows:])
    hidden = (gate / (1.0 + jnp.exp(-gate)) * up).astype(BF16)
    out_ref[...] = hidden
    half = part_ref.shape[1]
    part_ref[...] = jnp.where(lax.axis_index("tp") == 0, hidden[:, :half], hidden[:, half:])


def hidden_units(own, other):
    rows, units = own.shape
    return pl.pallas_call(
        hidden_kernel,
        in_specs=[WHOLE] * 2,
        out_specs=[WHOLE] * 2,
        out_shape=[
            jax.ShapeDtypeStruct((rows // 2, units), BF16),
            jax.ShapeDtypeStruct((rows // 2, units // 2), BF16),
        ],
        compiler_params=pltpu.CompilerParams(vmem_limit_bytes=8 * MIB),
        cost_estimate=cost(4 * own.size, 5 * own.size, own.size // 2),
        name="hidden_units",
    )(own, other)


def down_own_kernel(hidden_ref, down_ref, out_ref):
    units = hidden_ref.shape[1]
    first = pl.multiple_of(lax.axis_index("ctx") * units, units)
    out_ref[...] = jnp.dot(
        hidden_ref[...], down_ref[pl.ds(first, units), :], preferred_element_type=F32
    )


def other_product(part, down_ref, core):
    units = part.shape[1]
    first = pl.multiple_of((2 * (1 - lax.axis_index("ctx")) + core) * units, units)
    return jnp.dot(part, down_ref[pl.ds(first, units), :], preferred_element_type=F32)


def down_near_kernel(part_ref, down_ref, own_ref, out_ref):
    other = other_product(part_ref[...], down_ref, lax.axis_index("tp"))
    half = other.shape[0] // 2
    out_ref[...] = own_ref[...] + jnp.concatenate([other[half:], other[:half]])


def down_far_kernel(part_ref, down_ref, own_ref, out_ref):
    experts = lax.axis_size("exp")
    rows = out_ref.shape[1]
    other = other_product(part_ref[...], down_ref, 1 - lax.axis_index("tp"))
    half = other.shape[0] // 2
    total = (own_ref[...] + jnp.concatenate([other[half:], other[:half]])).astype(BF16)
    for block in range(out_ref.shape[0]):
        ctx = lax.axis_index("ctx") ^ (block // experts)
        exp = lax.axis_index("exp") ^ (block % experts)
        out_ref[ctx * experts + exp] = total[block * rows : (block + 1) * rows]


def down_sums(kernel, shape, dtype, hidden, down, *sums):
    rows, units = hidden.shape
    columns = down.shape[1]
    down = pltpu.with_memory_space_constraint(down, pltpu.VMEM)
    return pl.pallas_call(
        kernel,
        in_specs=[WHOLE] * (2 + len(sums)),
        out_specs=WHOLE,
        out_shape=jax.ShapeDtypeStruct(shape, dtype),
        compiler_params=pltpu.CompilerParams(vmem_limit_bytes=8 * MIB),
        cost_estimate=cost(2 * rows * units * columns, 2 * units * columns),
        name=kernel.__name__[:-7],
    )(hidden, down, *sums)


def merge_kernel(ids_ref, weight_ref, back_ref, out_ref, table):
    ctx_count, experts, rows, columns = back_ref.shape
    ids, weight = (ids_ref[...], weight_ref[...])
    for e in range(experts):
        table[e : e + 1, :rows] = jnp.sum(
            jnp.where(ids == e, weight, 0.0), axis=0, keepdims=True
        )
    share = jnp.transpose(table[...])
    for c in range(ctx_count):
        total = jnp.zeros((rows, columns), F32)
        for e in range(experts):
            total += share[:rows, e : e + 1] * back_ref[c, e].astype(F32)
        out_ref[:, c * columns : (c + 1) * columns] = total.astype(BF16)


def merge(route_ids, route_weight, back):
    ctx_count, experts, rows, columns = back.shape
    return pl.pallas_call(
        merge_kernel,
        in_specs=[WHOLE] * 3,
        out_specs=WHOLE,
        out_shape=jax.ShapeDtypeStruct((rows, ctx_count * columns), BF16),
        scratch_shapes=[pltpu.VMEM((8, 128), F32)],
        compiler_params=pltpu.CompilerParams(vmem_limit_bytes=8 * MIB),
        cost_estimate=cost(4 * back.size, 2 * back.size),
        name="merge",
    )(jnp.transpose(route_ids), jnp.transpose(route_weight), back)


def on_device(queries, keys, values, log_decay, moe_input, route_ids, route_weight, gate_up, down):
    ctx_count, expert_list = (lax.axis_size("ctx"), lax.axis_size("exp"))
    if (ctx_count, expert_list, lax.axis_size("tp")) != (2, 4, 2) or gate_up.shape[3] % 128:
        return on_device_any(
            queries, keys, values, log_decay, moe_input, route_ids, route_weight, gate_up, down
        )
    peers = ctx_count * expert_list
    swap = [(0, 1), (1, 0)]
    own_tokens = moe_input[None]
    moved = {
        d: lax.ppermute(own_tokens, "exp", [(e, e ^ d) for e in range(expert_list)])
        for d in range(expert_list - 1, 0, -1)
    }
    tokens = join(own_tokens, *(moved[d] for d in range(1, expert_list)))
    weights, w_down = (gate_up.reshape(gate_up.shape[1:]), down.reshape(down.shape[1:]))
    part = weights.shape[0] // 24
    intra, local, cum, held = attend(queries, keys, values, log_decay, weights, 8 * part)
    tokens, local = lax.optimization_barrier((tokens, local))
    held_next = hold(tokens, weights, 8 * part, 8 * part)
    far_tokens = lax.ppermute(tokens, "ctx", swap)
    sums = gate_up_sums(tokens, far_tokens, (held, held_next), weights)
    hidden, part = hidden_units(sums, lax.ppermute(sums, "tp", swap))
    part = lax.ppermute(part, "ctx", swap)
    sums_shape = (hidden.shape[0], w_down.shape[1])
    total = down_sums(down_own_kernel, sums_shape, F32, hidden, w_down)
    total, local = lax.optimization_barrier((total, local))
    state = lax.ppermute(local, "ctx", swap)
    part_far = lax.ppermute(part, "tp", swap)
    total = down_sums(down_near_kernel, sums_shape, F32, part, w_down, total)
    rows = moe_input.shape[0]
    expert_out = down_sums(
        down_far_kernel, (peers, rows, sums_shape[1]), BF16, part_far, w_down, total
    )
    back = lax.all_to_all(expert_out, ("ctx", "exp"), split_axis=0, concat_axis=0, tiled=True)
    attended = finish(queries, intra, cum, state)
    back = back.reshape((ctx_count, expert_list) + back.shape[1:])
    return (attended, merge(route_ids, route_weight, back))


def solution(mesh):
    in_specs = (
        P(("groups", "ctx"), ("exp", "tp")),
        P(("groups", "ctx"), ("exp", "tp")),
        P(("groups", "ctx"), ("exp", "tp")),
        P(("groups", "ctx"), ("exp", "tp")),
        P(("groups", "ctx", "exp"), "tp"),
        P(("groups", "ctx", "exp"), None),
        P(("groups", "ctx", "exp"), None),
        P("exp", "tp", None, "ctx"),
        P("exp", None, ("tp", "ctx")),
    )
    out_specs = (P(("groups", "ctx"), ("exp", "tp")), P(("groups", "ctx", "exp"), "tp"))
    return jax.shard_map(
        on_device, mesh=mesh, in_specs=in_specs, out_specs=out_specs, check_vma=False
    )
```

```python
import functools

import jax
import jax.numpy as jnp
from jax import lax
from jax.experimental import pallas as pl
from jax.experimental.pallas import tpu as pltpu
from jax.sharding import PartitionSpec as P

F32, BF16 = (jnp.float32, jnp.bfloat16)
WHOLE = pl.BlockSpec(memory_space=pltpu.VMEM)
SCALARS = pl.BlockSpec(memory_space=pltpu.SMEM)
THERE = pl.BlockSpec(memory_space=pl.ANY)
MIB = 1 << 20


def prefix(shard, axis, combine, identity):
    devices, here = (lax.axis_size(axis), lax.axis_index(axis))
    everything = jax.tree.map(
        lambda part, kind: lax.all_gather(part.astype(kind), axis),
        shard,
        (jnp.bfloat16, jnp.bfloat16),
    )
    start = jax.tree.map(
        lambda part, zero: jnp.broadcast_to(jnp.asarray(zero, part.dtype), part.shape),
        shard,
        identity,
    )

    def step(k, before):
        reached = k < here
        new = combine(
            before, jax.tree.map(lambda part, own: part[k].astype(own.dtype), everything, shard)
        )
        return jax.tree.map(lambda a, b: jnp.where(reached, a, b), new, before)

    return lax.fori_loop(0, devices, step, start)


def block_terms(queries, keys, values, log_decay):
    rows = queries.shape[0]
    heads = log_decay.shape[1]
    qb = queries.reshape(rows, heads, -1)
    kb = keys.reshape(rows, heads, -1)
    vb = values.reshape(rows, heads, -1)
    cum = jnp.cumsum(log_decay, axis=0)
    diff = jnp.transpose(cum)[:, :, None] - jnp.transpose(cum)[:, None, :]
    causal = jnp.arange(rows)[:, None] >= jnp.arange(rows)[None, :]
    decay = jnp.where(causal[None, :, :], jnp.exp(jnp.minimum(diff, 0.0)), 0.0)
    scores = jnp.einsum("thd,shd->hts", qb, kb, preferred_element_type=jnp.float32)
    weights = (scores * decay).astype(jnp.bfloat16)
    intra = jnp.einsum("hts,shd->thd", weights, vb, preferred_element_type=jnp.float32)
    last = cum[-1]
    kscaled = kb.astype(jnp.float32) * jnp.exp(last[None, :] - cum)[:, :, None]
    local = jnp.einsum(
        "shd,she->hde", kscaled, vb.astype(jnp.float32), precision=lax.Precision.HIGHEST
    )
    return (qb, cum, intra, local, jnp.exp(last))


def chain_states(preceding_positions, later):
    return (
        preceding_positions[0] * later[0],
        later[0][:, None, None] * preceding_positions[1] + later[1],
    )


def route_slots(route_ids, expert_list, slots_each):
    flat_ids = route_ids.reshape(-1)
    onehot = (flat_ids[:, None] == jnp.arange(expert_list)[None, :]).astype(jnp.int32)
    slot = jnp.sum((jnp.cumsum(onehot, axis=0) - 1) * onehot, axis=1)
    target = flat_ids * slots_each + slot
    pick = jnp.arange(expert_list * slots_each)[:, None] == target[None, :]
    return (target, pick)


def on_device_any(queries, keys, values, log_decay, moe_input, route_ids, route_weight, gate_up, down):
    qb, cum, intra, local, totals = block_terms(queries, keys, values, log_decay)
    heads = log_decay.shape[1]
    width = local.shape[1]
    identity = (jnp.ones((heads,), jnp.float32), jnp.zeros((heads, width, width), jnp.float32))
    entering = prefix((totals, local), "ctx", chain_states, identity)
    qscaled = qb.astype(jnp.float32) * jnp.exp(cum)[:, :, None]
    inter = jnp.einsum("thd,hde->the", qscaled, entering[1], precision=lax.Precision.HIGHEST)
    mixed = intra + inter
    normed = mixed * lax.rsqrt(jnp.mean(mixed * mixed, axis=-1, keepdims=True) + 1e-06)
    attended = normed.astype(jnp.bfloat16).reshape(queries.shape)
    expert_list = lax.axis_size("exp")
    ctx_count = lax.axis_size("ctx")
    tok_rows = moe_input.shape[0]
    half_width = moe_input.shape[1]
    slots_each = min(tok_rows, tok_rows * 2 // expert_list + tok_rows // 4)
    target, pick = route_slots(route_ids, expert_list, slots_each)
    doubled = jnp.repeat(moe_input, 2, axis=0)
    send = jnp.dot(pick.astype(jnp.bfloat16), doubled, preferred_element_type=jnp.float32)
    send = send.astype(jnp.bfloat16).reshape(expert_list, slots_each, half_width)
    arrived = lax.all_to_all(send, "exp", split_axis=0, concat_axis=0, tiled=True)
    slot_rows = arrived.reshape(expert_list * slots_each, half_width)
    w_both = gate_up.reshape(half_width, -1)
    ff_local = w_both.shape[1] // 2
    partial_value = jnp.dot(
        lax.all_gather(slot_rows, "ctx", axis=0, tiled=True),
        w_both,
        preferred_element_type=jnp.float32,
    )
    summed = lax.psum(partial_value.astype(jnp.bfloat16), "tp").astype(jnp.float32)
    hidden = (jax.nn.silu(summed[:, :ff_local]) * summed[:, ff_local:]).astype(jnp.bfloat16)
    w_down = down.reshape(down.shape[1], down.shape[2])
    expert_out = jnp.dot(
        lax.all_gather(hidden, "ctx", axis=1, tiled=True),
        w_down,
        preferred_element_type=jnp.float32,
    ).astype(jnp.bfloat16)
    col_width = expert_out.shape[1]
    stacked = expert_out.reshape(ctx_count, expert_list, slots_each, col_width)
    back = lax.all_to_all(
        lax.all_to_all(stacked, "ctx", split_axis=0, concat_axis=3, tiled=True),
        "exp",
        split_axis=1,
        concat_axis=1,
        tiled=True,
    )
    flat = back.reshape(expert_list * slots_each, half_width)
    selected_routes = flat[target].astype(jnp.float32).reshape(tok_rows, 2, half_width)
    merged_output = jnp.sum(selected_routes * route_weight[:, :, None], axis=1)
    return (attended, merged_output.astype(jnp.bfloat16))

def cost(flops, read, transcendentals=0):
    return pl.CostEstimate(flops=flops, bytes_accessed=read, transcendentals=transcendentals)


def head_columns(h, width):
    return slice(h * width, (h + 1) * width)


def attend_kernel(
    heads, q_hbm, k_hbm, v_hbm, decay_hbm, weights_hbm, intra_ref, local_ref, cum_ref, held_ref,
    q_ref, k_ref, v_ref, decay_ref, sems,
):
    pairs = (
        (decay_hbm, decay_ref),
        (q_hbm, q_ref),
        (k_hbm, k_ref),
        (v_hbm, v_ref),
        (weights_hbm.at[pl.ds(0, held_ref.shape[0])], held_ref),
    )
    fetches = [pltpu.make_async_copy(a, b, sems.at[i]) for i, (a, b) in enumerate(pairs)]
    for fetch in fetches:
        fetch.start()
    rows = q_ref.shape[0]
    width = q_ref.shape[1] // heads
    s_at = lax.broadcasted_iota(jnp.int32, (rows, rows), 0)
    t_at = lax.broadcasted_iota(jnp.int32, (rows, rows), 1)
    before = (s_at <= t_at).astype(F32)
    fetches[0].wait()
    cum_t = jnp.dot(
        decay_ref[...], before, precision=lax.Precision.HIGHEST, preferred_element_type=F32
    )
    cum = jnp.transpose(cum_t)
    cum_ref[...] = cum
    for fetch in fetches[1:4]:
        fetch.wait()
    for h in range(heads):
        at = head_columns(h, width)
        q, k, v = (q_ref[:, at], k_ref[:, at], v_ref[:, at])
        column, row = (cum[:, h : h + 1], cum_t[h : h + 1, :])
        decay = jnp.where(s_at >= t_at, jnp.exp(jnp.minimum(column - row, 0.0)), 0.0)
        scores = lax.dot_general(q, k, (((1,), (1,)), ((), ())), preferred_element_type=F32)
        intra_ref[:, at] = jnp.dot(
            (scores * decay).astype(BF16), v, preferred_element_type=F32
        )
        rest = jnp.exp(cum[rows - 1 :, h : h + 1] - column)
        scaled = (k.astype(F32) * rest).astype(BF16)
        local = lax.dot_general(scaled, v, (((0,), (0,)), ((), ())), preferred_element_type=F32)
        local_ref[h * width : (h + 1) * width, :] = local.astype(BF16)
    fetches[4].wait()


def attend(queries, keys, values, log_decay, weights, depth):
    rows, heads = log_decay.shape
    width = queries.shape[1] // heads
    operands = (queries, keys, values, jnp.transpose(log_decay), weights)
    return pl.pallas_call(
        functools.partial(attend_kernel, heads),
        in_specs=[THERE] * 5,
        out_specs=[WHOLE] * 4,
        out_shape=[
            jax.ShapeDtypeStruct(queries.shape, F32),
            jax.ShapeDtypeStruct((heads * width, width), BF16),
            jax.ShapeDtypeStruct((rows, heads), F32),
            pltpu.VMEM((depth,) + weights.shape[1:], BF16),
        ],
        scratch_shapes=[pltpu.VMEM(queries.shape, BF16)] * 3
        + [pltpu.VMEM((heads, rows), F32), pltpu.SemaphoreType.DMA((5,))],
        compiler_params=pltpu.CompilerParams(vmem_limit_bytes=8 * MIB),
        cost_estimate=cost(10**10, 6 * queries.size, heads * rows * rows),
        name="attend",
    )(*(pltpu.with_memory_space_constraint(x, pltpu.HBM) for x in operands))


def finish_kernel(heads, q_ref, intra_ref, cum_ref, state_ref, out_ref):
    width = q_ref.shape[1] // heads
    entered = lax.axis_index("ctx") > 0
    for h in range(heads):
        at = head_columns(h, width)
        grown = jnp.where(entered, jnp.exp(cum_ref[:, h : h + 1]), 0.0)
        state = state_ref[h * width : (h + 1) * width, :]
        mixed = intra_ref[:, at] + grown * jnp.dot(
            q_ref[:, at], state, preferred_element_type=F32
        )
        mean = jnp.mean(mixed * mixed, axis=1, keepdims=True)
        out_ref[:, at] = (mixed * lax.rsqrt(mean + 1e-06)).astype(BF16)


def finish(queries, intra, cum, state):
    rows, heads = cum.shape
    return pl.pallas_call(
        functools.partial(finish_kernel, heads),
        in_specs=[WHOLE] * 4,
        out_specs=WHOLE,
        out_shape=jax.ShapeDtypeStruct(queries.shape, BF16),
        compiler_params=pltpu.CompilerParams(vmem_limit_bytes=8 * MIB),
        cost_estimate=cost(2 * queries.size * 128, 10 * queries.size, queries.size),
        name="finish",
    )(queries, intra, cum, state)


def join_kernel(*refs):
    out_ref = refs[-1]
    for i, part_ref in enumerate(refs[:-1]):
        out_ref[i : i + 1] = part_ref[...]


def join(*parts):
    return pl.pallas_call(
        join_kernel,
        in_specs=[WHOLE] * len(parts),
        out_specs=WHOLE,
        out_shape=jax.ShapeDtypeStruct((len(parts),) + parts[0].shape[1:], parts[0].dtype),
        compiler_params=pltpu.CompilerParams(vmem_limit_bytes=4 * MIB),
        cost_estimate=cost(0, 16 * parts[0].size),
        name="join",
    )(*parts)


def hold_kernel(first, after_ref, weights_hbm, held_ref, sem):
    fetch = pltpu.make_async_copy(
        weights_hbm.at[pl.ds(first, held_ref.shape[0])], held_ref, sem
    )
    fetch.start()
    fetch.wait()


def hold(after, weights, first, depth):
    return pl.pallas_call(
        functools.partial(hold_kernel, first),
        in_specs=[THERE, THERE],
        out_specs=WHOLE,
        out_shape=pltpu.VMEM((depth,) + weights.shape[1:], BF16),
        scratch_shapes=[pltpu.SemaphoreType.DMA],
        compiler_params=pltpu.CompilerParams(vmem_limit_bytes=4 * MIB),
        cost_estimate=cost(0, 2 * depth * weights.shape[1] * weights.shape[2]),
        name="hold",
    )(after, pltpu.with_memory_space_constraint(weights, pltpu.HBM))


def gate_up_kernel(
    near_ref, far_ref, a_ref, b_ref, weights_hbm, sums_ref, spread, last_ref, sem
):
    held = (a_ref, b_ref, last_ref)
    first = sum(part.shape[0] for part in held[:-1])
    fetch = pltpu.make_async_copy(
        weights_hbm.at[pl.ds(first, last_ref.shape[0])], last_ref, sem
    )
    fetch.start()
    depth, _, units = weights_hbm.shape
    rows = near_ref.shape[0] * near_ref.shape[1]
    lanes = 128
    source = lax.broadcasted_iota(jnp.int32, (lanes, 4 * lanes), 0)
    goal = lax.broadcasted_iota(jnp.int32, (lanes, 4 * lanes), 1)
    places = jnp.where(goal < 2 * lanes, 2 * source, 2 * source + 2 * lanes + 1)
    x = jnp.concatenate([near_ref[...].reshape(rows, depth), far_ref[...].reshape(rows, depth)])
    rows = 2 * rows
    blocks = depth // lanes
    stacked = jnp.concatenate([x[:, b * lanes : (b + 1) * lanes] for b in range(blocks)])
    wide = jnp.dot(stacked, (goal == places).astype(BF16), preferred_element_type=F32)
    wide = wide.astype(BF16)
    for b in range(blocks):
        to = slice(2 * b * lanes, 2 * (b + 1) * lanes)
        spread[:rows, to] = wide[b * rows : (b + 1) * rows, : 2 * lanes]
        spread[rows:, to] = wide[b * rows : (b + 1) * rows, 2 * lanes :]
    total = jnp.zeros((2 * rows, units), F32)
    start = 0
    for part in held:
        if part is last_ref:
            fetch.wait()
        end = start + 2 * part.shape[0]
        total += jnp.dot(
            spread[:, start:end],
            part[...].reshape(end - start, units),
            preferred_element_type=F32,
        )
        start = end
    sums_ref[...] = total.astype(BF16)


def gate_up_sums(near, far, held, weights):
    rows = 2 * near.shape[0] * near.shape[1]
    depth, _, units = weights.shape
    rest = depth - sum(part.shape[0] for part in held)
    held = [pltpu.with_memory_space_constraint(part, pltpu.VMEM) for part in held]
    return pl.pallas_call(
        gate_up_kernel,
        in_specs=[WHOLE] * 4 + [THERE],
        out_specs=WHOLE,
        out_shape=jax.ShapeDtypeStruct((2 * rows, units), BF16),
        scratch_shapes=[
            pltpu.VMEM((2 * rows, 2 * depth), BF16),
            pltpu.VMEM((rest,) + weights.shape[1:], BF16),
            pltpu.SemaphoreType.DMA,
        ],
        compiler_params=pltpu.CompilerParams(vmem_limit_bytes=20 * MIB),
        cost_estimate=cost(4 * rows * weights.size, 2 * weights.size),
        name="gate_up_sums",
    )(near, far, *held, pltpu.with_memory_space_constraint(weights, pltpu.HBM))


def hidden_kernel(own_ref, other_ref, out_ref, part_ref):
    rows = out_ref.shape[0]
    summed = own_ref[...].astype(F32) + other_ref[...].astype(F32)
    gate, up = (summed[:rows], summed[rows:])
    hidden = (gate / (1.0 + jnp.exp(-gate)) * up).astype(BF16)
    out_ref[...] = hidden
    half = part_ref.shape[1]
    part_ref[...] = jnp.where(lax.axis_index("tp") == 0, hidden[:, :half], hidden[:, half:])


def hidden_units(own, other):
    rows, units = own.shape
    return pl.pallas_call(
        hidden_kernel,
        in_specs=[WHOLE] * 2,
        out_specs=[WHOLE] * 2,
        out_shape=[
            jax.ShapeDtypeStruct((rows // 2, units), BF16),
            jax.ShapeDtypeStruct((rows // 2, units // 2), BF16),
        ],
        compiler_params=pltpu.CompilerParams(vmem_limit_bytes=8 * MIB),
        cost_estimate=cost(4 * own.size, 5 * own.size, own.size // 2),
        name="hidden_units",
    )(own, other)


def down_own_kernel(hidden_ref, down_ref, out_ref):
    units = hidden_ref.shape[1]
    first = pl.multiple_of(lax.axis_index("ctx") * units, units)
    out_ref[...] = jnp.dot(
        hidden_ref[...], down_ref[pl.ds(first, units), :], preferred_element_type=F32
    )


def other_product(part, down_ref, core):
    units = part.shape[1]
    first = pl.multiple_of((2 * (1 - lax.axis_index("ctx")) + core) * units, units)
    return jnp.dot(part, down_ref[pl.ds(first, units), :], preferred_element_type=F32)


def down_near_kernel(part_ref, down_ref, own_ref, out_ref):
    other = other_product(part_ref[...], down_ref, lax.axis_index("tp"))
    half = other.shape[0] // 2
    out_ref[...] = own_ref[...] + jnp.concatenate([other[half:], other[:half]])


def down_far_kernel(part_ref, down_ref, own_ref, out_ref):
    experts = lax.axis_size("exp")
    rows = out_ref.shape[1]
    other = other_product(part_ref[...], down_ref, 1 - lax.axis_index("tp"))
    half = other.shape[0] // 2
    total = (own_ref[...] + jnp.concatenate([other[half:], other[:half]])).astype(BF16)
    for block in range(out_ref.shape[0]):
        ctx = lax.axis_index("ctx") ^ (block // experts)
        exp = lax.axis_index("exp") ^ (block % experts)
        out_ref[ctx * experts + exp] = total[block * rows : (block + 1) * rows]


def down_sums(kernel, shape, dtype, hidden, down, *sums):
    rows, units = hidden.shape
    columns = down.shape[1]
    down = pltpu.with_memory_space_constraint(down, pltpu.VMEM)
    return pl.pallas_call(
        kernel,
        in_specs=[WHOLE] * (2 + len(sums)),
        out_specs=WHOLE,
        out_shape=jax.ShapeDtypeStruct(shape, dtype),
        compiler_params=pltpu.CompilerParams(vmem_limit_bytes=8 * MIB),
        cost_estimate=cost(2 * rows * units * columns, 2 * units * columns),
        name=kernel.__name__[:-7],
    )(hidden, down, *sums)


def merge_kernel(ids_ref, weight_ref, back_ref, out_ref, table):
    ctx_count, experts, rows, columns = back_ref.shape
    ids, weight = (ids_ref[...], weight_ref[...])
    for e in range(experts):
        table[e : e + 1, :rows] = jnp.sum(
            jnp.where(ids == e, weight, 0.0), axis=0, keepdims=True
        )
    share = jnp.transpose(table[...])
    for c in range(ctx_count):
        total = jnp.zeros((rows, columns), F32)
        for e in range(experts):
            total += share[:rows, e : e + 1] * back_ref[c, e].astype(F32)
        out_ref[:, c * columns : (c + 1) * columns] = total.astype(BF16)


def merge(route_ids, route_weight, back):
    ctx_count, experts, rows, columns = back.shape
    return pl.pallas_call(
        merge_kernel,
        in_specs=[WHOLE] * 3,
        out_specs=WHOLE,
        out_shape=jax.ShapeDtypeStruct((rows, ctx_count * columns), BF16),
        scratch_shapes=[pltpu.VMEM((8, 128), F32)],
        compiler_params=pltpu.CompilerParams(vmem_limit_bytes=8 * MIB),
        cost_estimate=cost(4 * back.size, 2 * back.size),
        name="merge",
    )(jnp.transpose(route_ids), jnp.transpose(route_weight), back)


def on_device(queries, keys, values, log_decay, moe_input, route_ids, route_weight, gate_up, down):
    ctx_count, expert_list = (lax.axis_size("ctx"), lax.axis_size("exp"))
    if (ctx_count, expert_list, lax.axis_size("tp")) != (2, 4, 2) or gate_up.shape[3] % 128:
        return on_device_any(
            queries, keys, values, log_decay, moe_input, route_ids, route_weight, gate_up, down
        )
    peers = ctx_count * expert_list
    swap = [(0, 1), (1, 0)]
    own_tokens = moe_input[None]
    moved = {
        d: lax.ppermute(own_tokens, "exp", [(e, e ^ d) for e in range(expert_list)])
        for d in (3, 1, 2)
    }
    tokens = join(own_tokens, *(moved[d] for d in range(1, expert_list)))
    weights, w_down = (gate_up.reshape(gate_up.shape[1:]), down.reshape(down.shape[1:]))
    part = weights.shape[0] // 24
    intra, local, cum, held = attend(queries, keys, values, log_decay, weights, 8 * part)
    tokens, local = lax.optimization_barrier((tokens, local))
    held_next = hold(tokens, weights, 8 * part, 8 * part)
    far_tokens = lax.ppermute(tokens, "ctx", swap)
    sums = gate_up_sums(tokens, far_tokens, (held, held_next), weights)
    hidden, part = hidden_units(sums, lax.ppermute(sums, "tp", swap))
    part = lax.ppermute(part, "ctx", swap)
    sums_shape = (hidden.shape[0], w_down.shape[1])
    total = down_sums(down_own_kernel, sums_shape, F32, hidden, w_down)
    total, local = lax.optimization_barrier((total, local))
    state = lax.ppermute(local, "ctx", swap)
    part_far = lax.ppermute(part, "tp", swap)
    total = down_sums(down_near_kernel, sums_shape, F32, part, w_down, total)
    rows = moe_input.shape[0]
    expert_out = down_sums(
        down_far_kernel, (peers, rows, sums_shape[1]), BF16, part_far, w_down, total
    )
    back = lax.all_to_all(expert_out, ("ctx", "exp"), split_axis=0, concat_axis=0, tiled=True)
    attended = finish(queries, intra, cum, state)
    back = back.reshape((ctx_count, expert_list) + back.shape[1:])
    return (attended, merge(route_ids, route_weight, back))


def solution(mesh):
    in_specs = (
        P(("groups", "ctx"), ("exp", "tp")),
        P(("groups", "ctx"), ("exp", "tp")),
        P(("groups", "ctx"), ("exp", "tp")),
        P(("groups", "ctx"), ("exp", "tp")),
        P(("groups", "ctx", "exp"), "tp"),
        P(("groups", "ctx", "exp"), None),
        P(("groups", "ctx", "exp"), None),
        P("exp", "tp", None, "ctx"),
        P("exp", None, ("tp", "ctx")),
    )
    out_specs = (P(("groups", "ctx"), ("exp", "tp")), P(("groups", "ctx", "exp"), "tp"))
    return jax.shard_map(
        on_device, mesh=mesh, in_specs=in_specs, out_specs=out_specs, check_vma=False
    )
```
